512 devices in a mesh: seq: 32 (over y, x), rep: 16 (over z, core).
Axes of the slice: x: 4, y: 8, z: 8, core: 2. Of those that a mesh axis runs over, the one named last changes fastest.
Arguments:
- histories: bfloat16 [16, 32, 6, 64, 512], P('rep', 'seq'), may hold values from -6 to 6
- cotangents: bfloat16 [16, 32, 6, 64, 512], P('rep', 'seq'), may hold values from -6 to 6
- lengths: int32 [16, 32, 6], P('rep', 'seq'), may hold values from 0 to 64, as said below
- w_in: bfloat16 [512, 2048], replicated, may hold values from -0.25 to 0.25
- w_out: bfloat16 [512, 512], replicated, may hold values from -0.25 to 0.25
Outputs:
- input_grads: bfloat16 [16, 32, 6, 64, 512], P('rep', 'seq')
- w_in_grad: float32 [512, 2048], P('rep', 'seq')
The draws below stay inside these ranges and needn't reach their ends.
Inputs may be any that keep to these rules, and one draw needn't show every extreme that they name: `lengths`: in each replica group exactly 64 slots have a positive length, every live length is at least 8, and in each group some rank has all 6 of its slots live.
All inputs are finite; a program needn't handle non-finite values.
Results may differ from the reference program's by a relative error of at most 0.025.
Values may be sent and summed in bfloat16 or wider, within the bound.
No kernel may reach another device: no remote copies, remote signals or barrier semaphores. Data moves between devices by JAX's collectives and lax.ppermute only.
A program may use at most 64 MiB of HBM per device.

```python
import jax
import jax.numpy as jnp
from jax import lax

D = 512
HEADS = 8
MAXLEN = 64
HOME = 6
CAP = 2
REPLICAS = 16
RANKS = 32
N_SEQ = 32
N_REP = 16


def draw_lengths(key, part):

    def one_group(group_key):
        slot_total = RANKS * HOME
        keys_list = jax.random.split(group_key, 4)
        shuffled = jax.random.permutation(keys_list[0], slot_total).astype(jnp.int32)
        heavy_rank = jax.random.randint(keys_list[1], (), 0, RANKS)
        slot_index = jnp.arange(slot_total, dtype=jnp.int32)
        ranking = shuffled - jnp.where(slot_index // HOME == heavy_rank, slot_total, 0)
        ordered = jnp.argsort(ranking)
        is_live = jnp.zeros(slot_total, jnp.int32).at[ordered[:CAP * RANKS]].set(1)
        lowest = MAXLEN // 8
        first_draw = jax.random.randint(keys_list[2], (slot_total,), 0, MAXLEN - lowest + 1)
        second_draw = jax.random.randint(keys_list[3], (slot_total,), 0, MAXLEN - lowest + 1)
        sizes = MAXLEN - first_draw * second_draw // (MAXLEN - lowest)
        return (sizes * is_live).astype(jnp.int32).reshape(RANKS, HOME)
    group_keys = jax.random.split(jax.random.fold_in(key, 11), REPLICAS)
    return jax.vmap(one_group)(group_keys)


def block_levels(stream_key, dims, cuts, low, largest):
    level = 1.0
    for axis_at, blocks in cuts:
        heights = jax.random.uniform(jax.random.fold_in(jax.random.fold_in(stream_key, 6), axis_at), (blocks,), jnp.float32, low / len(cuts), largest / len(cuts))
        level = level * jnp.repeat(jnp.exp(heights), dims[axis_at] // blocks).reshape((-1,) + (1,) * (len(dims) - 1 - axis_at))
    return level


def centred(own_key, dims, scale, reach, cuts=(), kind=jnp.bfloat16):
    result = scale * jax.random.normal(own_key, dims, jnp.float32)
    if cuts:
        result = result * block_levels(own_key, dims, cuts, -0.22, 0.18)
    return jnp.clip(result, -reach, reach).astype(kind)


def setup_inputs(seed: int = 0) -> dict:
    streams_of = jax.random.split(jax.random.key(seed), 6)
    return {
        "histories": centred(streams_of[0], (REPLICAS, RANKS, HOME, MAXLEN, D), 1.0, 6.0, ((0, 16), (1, 32))),
        "cotangents": centred(streams_of[1], (REPLICAS, RANKS, HOME, MAXLEN, D), 1.0, 6.0, ((0, 16), (1, 32))),
        "lengths": draw_lengths(jax.random.fold_in(streams_of[5], 71), 0),
        "w_in": centred(streams_of[3], (D, 4 * D), D ** -0.5, 0.25),
        "w_out": centred(streams_of[4], (D, D), D ** -0.5, 0.25),
    }


def layer_norm(values):
    average = lax.optimization_barrier(jnp.mean(values, axis=-1, keepdims=True))
    centered = values - average
    spread = lax.optimization_barrier(jnp.mean(centered * centered, axis=-1, keepdims=True))
    return centered * lax.rsqrt(spread + 1e-06)

def forward(history, weight_in, weight_out, lengths):
    count_slots, positions, features = history.shape
    head_size = features // HEADS
    normed = layer_norm(history.astype(jnp.float32)).astype(jnp.bfloat16)
    projected = jax.nn.silu(jnp.dot(normed.reshape(count_slots * positions, features), weight_in, preferred_element_type=jnp.float32)).astype(jnp.bfloat16)
    projected = projected.reshape(count_slots, positions, 4, HEADS, head_size)
    gate_rows = projected[:, :, 0].reshape(count_slots, positions, features)
    value_rows = projected[:, :, 1]
    query_rows = projected[:, :, 2]
    key_rows = projected[:, :, 3]
    scores = jnp.einsum('cthe,cshe->chts', query_rows, key_rows, preferred_element_type=jnp.float32) * head_size ** (-0.5)
    row_ids = jnp.arange(positions, dtype=jnp.int32)
    allowed = (row_ids[None, :] <= row_ids[:, None])[None, None] & (row_ids[None, None, None, :] < lengths[:, None, None, None])
    weights = (jnp.where(allowed, jax.nn.silu(scores), 0.0) / lengths.astype(jnp.float32)[:, None, None, None]).astype(jnp.bfloat16)
    attended = jnp.einsum('chts,cshe->cthe', weights, value_rows, preferred_element_type=jnp.float32).reshape(count_slots, positions, features)
    gated_out = (layer_norm(attended) * gate_rows.astype(jnp.float32)).astype(jnp.bfloat16)
    mixed_out = jnp.dot(gated_out.reshape(count_slots * positions, features), weight_out, preferred_element_type=jnp.float32)
    return history.astype(jnp.float32) + mixed_out.reshape(count_slots, positions, features)

def cotangent_seed(cotangent, lengths):
    row_ids = jnp.arange(cotangent.shape[1], dtype=jnp.int32)
    valid = row_ids[None, :] < lengths[:, None]
    return jnp.where(valid[:, :, None], cotangent.astype(jnp.float32), 0.0)

def assign(flat_lengths, devices, home_slots):
    slot_total = devices * home_slots
    slot_index = jnp.arange(slot_total, dtype=jnp.int32)
    is_live = flat_lengths > 0
    work_cost = flat_lengths * flat_lengths
    ranking = jnp.where(is_live, slot_index - work_cost * slot_total, slot_total * slot_total + slot_index)
    ordered = jnp.argsort(ranking).astype(jnp.int32)
    leading = ordered[:devices]
    trailing = ordered[devices:2 * devices][::-1]
    device_ids = jnp.arange(devices, dtype=jnp.int32)
    partner_ids = trailing[(device_ids[None, :] + device_ids[:, None]) % devices]
    clashes = jnp.any(leading[None, :] // home_slots == partner_ids // home_slots, axis=1)
    chosen_shift = jnp.argmin(jnp.where(clashes, devices + device_ids, device_ids)).astype(jnp.int32)
    usable = jnp.logical_not(jnp.all(clashes))
    partners = trailing[(device_ids + chosen_shift) % devices]
    paired_dest = jnp.zeros(slot_total, jnp.int32).at[leading].set(device_ids).at[partners].set(device_ids)
    paired_slot = jnp.zeros(slot_total, jnp.int32).at[partners].set(1)
    position = jnp.cumsum(is_live.astype(jnp.int32)).astype(jnp.int32) - 1
    destination = jnp.where(is_live, jnp.where(usable, paired_dest, position % devices), -1)
    arrival = jnp.where(is_live, jnp.where(usable, paired_slot, position // devices), -1)
    return (destination, arrival)

def reference(histories, cotangents, lengths, w_in, w_out):
    devices = N_SEQ
    groups = N_REP
    slot_total = devices * HOME
    flat_hist = histories.reshape(groups * slot_total, MAXLEN, D)
    flat_cot = cotangents.reshape(groups * slot_total, MAXLEN, D)
    flat_lengths = lengths.reshape(groups, slot_total)
    destination, arrival = jax.vmap(lambda lengths_row: assign(lengths_row, devices, HOME))(flat_lengths)
    slot_index = jnp.arange(slot_total, dtype=jnp.int32)
    selected = (destination[:, None, None, :] == jnp.arange(devices, dtype=jnp.int32)[None, :, None, None]) & (arrival[:, None, None, :] == jnp.arange(CAP, dtype=jnp.int32)[None, None, :, None])
    members = lax.optimization_barrier(jnp.sum(jnp.where(selected, slot_index, 0), axis=3)).astype(jnp.int32)
    group_ids = jnp.repeat(jnp.arange(groups, dtype=jnp.int32), devices)
    members_flat = members.reshape(groups * devices, CAP)
    lengths_all = flat_lengths.reshape(groups * slot_total)

    def one_device(total, item):
        group_id, picked = item
        rows_at = group_id * slot_total + picked
        history = flat_hist[rows_at]
        cotangent = flat_cot[rows_at]
        picked_lengths = lengths_all[rows_at]
        _, pullback = jax.vjp(lambda history_in, weight_in: forward(history_in, weight_in, w_out, picked_lengths), history, w_in)
        grad_hist, grad_in = pullback(cotangent_seed(cotangent, picked_lengths))
        return (total + grad_in.astype(jnp.float32), grad_hist)
    total, grads = lax.scan(one_device, jnp.zeros((D, 4 * D), jnp.float32), (group_ids, members_flat))
    home_index = jnp.arange(groups, dtype=jnp.int32)[:, None] * (devices * CAP) + destination * CAP + arrival
    home = grads.reshape(groups * devices * CAP, MAXLEN, D)[jnp.clip(home_index, 0, groups * devices * CAP - 1)]
    home = jnp.where((flat_lengths > 0)[:, :, None, None], home, jnp.zeros((), home.dtype)).astype(jnp.bfloat16)
    return (home.reshape(histories.shape), total)
```

```python
import jax
import jax.numpy as jnp
from jax import lax
from jax.sharding import Mesh
from jax.sharding import PartitionSpec as P

HEADS = 8
CAP = 2
REP = ("rep_0", "rep_1")


def sent_to_all(shard, axis):
    copies = jnp.broadcast_to(shard, (lax.axis_size(axis), *shard.shape))
    return lax.all_to_all(copies, axis, split_axis=0, concat_axis=0, tiled=True)


def laid_out(tiles, dim):
    shape = list(tiles.shape[1:])
    shape[dim] *= tiles.shape[0]
    return jnp.moveaxis(tiles, 0, dim).reshape(shape)


def gather_directly(shard, axis, dim):
    tiles = sent_to_all(shard, axis)
    return laid_out(tiles, dim)


def cut_along(shard, dim, count):
    before, after = (shard.shape[:dim], shard.shape[dim + 1 :])
    return jnp.moveaxis(shard.reshape(*before, count, -1, *after), dim, 0)


def sum_by_chip(shard, chips, core, dim):
    sizes = (lax.axis_size(chips), lax.axis_size(core))
    tiles = cut_along(shard, dim, sizes[0] * sizes[1])
    inside = tiles.shape[1:]
    tiles = tiles.reshape(*sizes, *inside).swapaxes(0, 1).reshape(-1, *inside)
    tiles = lax.psum_scatter(tiles, core, scatter_dimension=0, tiled=True)
    return lax.psum_scatter(tiles, chips, scatter_dimension=0, tiled=True)[0]


def sum_at_owner(shard, axis, dim):
    count = lax.axis_size(axis)
    tiles = lax.all_to_all(cut_along(shard, dim, count), axis, 0, 0, tiled=True)
    return jnp.sum(tiles.astype(jnp.float32), axis=0)


def layer_norm(values):
    average = jnp.mean(values, axis=-1, keepdims=True)
    centered = values - average
    spread = jnp.mean(centered * centered, axis=-1, keepdims=True)
    return centered * lax.rsqrt(spread + 1e-06)


def forward(history, weight_in, weight_out, lengths):
    count_slots, positions, features = history.shape
    head_size = features // HEADS
    normed = layer_norm(history.astype(jnp.float32)).astype(jnp.bfloat16)
    projected = jax.nn.silu(
        jnp.dot(
            normed.reshape(count_slots * positions, features),
            weight_in,
            preferred_element_type=jnp.float32,
        )
    ).astype(jnp.bfloat16)
    projected = projected.reshape(count_slots, positions, 4, HEADS, head_size)
    gate_rows = projected[:, :, 0].reshape(count_slots, positions, features)
    value_rows = projected[:, :, 1]
    query_rows = projected[:, :, 2]
    key_rows = projected[:, :, 3]
    scores = jnp.einsum(
        "cthe,cshe->chts", query_rows, key_rows, preferred_element_type=jnp.float32
    ) * head_size ** (-0.5)
    row_ids = jnp.arange(positions, dtype=jnp.int32)
    allowed = (row_ids[None, :] <= row_ids[:, None])[None, None] & (
        row_ids[None, None, None, :] < lengths[:, None, None, None]
    )
    weights = (
        jnp.where(allowed, jax.nn.silu(scores), 0.0)
        / lengths.astype(jnp.float32)[:, None, None, None]
    ).astype(jnp.bfloat16)
    attended = jnp.einsum(
        "chts,cshe->cthe", weights, value_rows, preferred_element_type=jnp.float32
    ).reshape(count_slots, positions, features)
    gated_out = (layer_norm(attended) * gate_rows.astype(jnp.float32)).astype(jnp.bfloat16)
    mixed_out = jnp.dot(
        gated_out.reshape(count_slots * positions, features),
        weight_out,
        preferred_element_type=jnp.float32,
    )
    return history.astype(jnp.float32) + mixed_out.reshape(count_slots, positions, features)


def cotangent_seed(cotangent, lengths):
    row_ids = jnp.arange(cotangent.shape[1], dtype=jnp.int32)
    valid = row_ids[None, :] < lengths[:, None]
    return jnp.where(valid[:, :, None], cotangent.astype(jnp.float32), 0.0)


def assign(flat_lengths, devices, home_slots):
    slot_total = devices * home_slots
    slot_index = jnp.arange(slot_total, dtype=jnp.int32)
    is_live = flat_lengths > 0
    work_cost = flat_lengths * flat_lengths
    ranking = jnp.where(
        is_live, slot_index - work_cost * slot_total, slot_total * slot_total + slot_index
    )
    ordered = jnp.argsort(ranking)
    leading = ordered[:devices]
    trailing = ordered[devices : 2 * devices][::-1]
    device_ids = jnp.arange(devices, dtype=jnp.int32)
    partner_ids = trailing[(device_ids[None, :] + device_ids[:, None]) % devices]
    clashes = jnp.any(leading[None, :] // home_slots == partner_ids // home_slots, axis=1)
    chosen_shift = jnp.argmin(jnp.where(clashes, devices + device_ids, device_ids))
    usable = jnp.logical_not(jnp.all(clashes))
    partners = trailing[(device_ids + chosen_shift) % devices]
    paired_dest = (
        jnp.zeros(slot_total, jnp.int32).at[leading].set(device_ids).at[partners].set(device_ids)
    )
    paired_slot = jnp.zeros(slot_total, jnp.int32).at[partners].set(1)
    position = jnp.sum((is_live[None, :] & (slot_index[None, :] < slot_index[:, None])).astype(jnp.int32), axis=1)
    destination = jnp.where(is_live, jnp.where(usable, paired_dest, position % devices), -1)
    arrival = jnp.where(is_live, jnp.where(usable, paired_slot, position // devices), -1)
    return (destination, arrival)


def shards(histories, cotangents, lengths, w_in, w_out):
    home_slots = histories.shape[2]
    positions = histories.shape[3]
    features = histories.shape[4]
    devices = lax.axis_size("seq")
    device_index = lax.axis_index("seq")
    every_length = gather_directly(lengths, "seq", 1)
    flat_lengths = every_length.reshape(devices * home_slots)
    destination, arrival = assign(flat_lengths, devices, home_slots)
    my_dest = lax.dynamic_slice_in_dim(destination, device_index * home_slots, home_slots)
    device_ids = jnp.arange(devices, dtype=jnp.int32)
    routing = (my_dest[None, :] == device_ids[:, None]).astype(jnp.bfloat16)
    slot_index = jnp.arange(devices * home_slots, dtype=jnp.int32)
    selected = (destination[None, :] == device_index) & (
        arrival[None, :] == jnp.arange(CAP, dtype=jnp.int32)[:, None]
    )
    arriving = jnp.sum(jnp.where(selected, slot_index[None, :], 0), axis=1)
    arriving_length = flat_lengths[arriving]
    chooser = ((arriving // home_slots)[:, None] == device_ids[None, :]).astype(jnp.bfloat16)

    def outgoing(source):
        spread_out = jnp.dot(
            routing,
            source.reshape(home_slots, positions * features),
            preferred_element_type=jnp.bfloat16,
        )
        return spread_out.reshape(devices, positions, features)

    def collect(source):
        gathered = jnp.dot(
            chooser,
            source.reshape(devices, positions * features),
            preferred_element_type=jnp.bfloat16,
        )
        return gathered.reshape(CAP, positions, features)

    received = lax.all_to_all(outgoing(histories), "seq", split_axis=0, concat_axis=0, tiled=True)
    local_hist = collect(received)
    _, pullback = jax.vjp(
        lambda history_in, weight_in: forward(history_in, weight_in, w_out, arriving_length),
        local_hist,
        w_in,
    )
    local_cot = collect(
        lax.all_to_all(outgoing(cotangents), "seq", split_axis=0, concat_axis=0, tiled=True)
    )
    grad_hist, grad_in = pullback(cotangent_seed(local_cot, arriving_length))
    going_back = jnp.dot(
        chooser.T, grad_hist.reshape(CAP, positions * features), preferred_element_type=jnp.bfloat16
    )
    going_back = going_back.reshape(devices, positions, features)
    returned = lax.all_to_all(going_back, "seq", split_axis=0, concat_axis=0, tiled=True)
    home_grad = jnp.dot(
        routing.T,
        returned.reshape(devices, positions * features),
        preferred_element_type=jnp.bfloat16,
    )
    home_grad = home_grad.reshape(histories.shape)
    gradient = grad_in.astype(jnp.float32)
    row_block = sum_by_chip(gradient.astype(jnp.bfloat16), "rep_0", "rep_1", 0).astype(jnp.float32)
    w_in_grad = sum_at_owner(row_block.astype(jnp.bfloat16), "seq", 1)
    return (home_grad, w_in_grad)


def solution(mesh):
    torus = Mesh(mesh.devices.reshape(mesh.shape["seq"], 8, 2), ("seq", "rep_0", "rep_1"))
    placed = (
        P(REP, "seq", None, None, None),
        P(REP, "seq", None, None, None),
        P(REP, "seq", None),
        P(),
        P(),
    )
    return jax.shard_map(
        shards,
        mesh=torus,
        in_specs=placed,
        out_specs=(P(REP, "seq", None, None, None), P(REP, "seq")),
        check_vma=False,
    )
```

```python
import jax
import jax.numpy as jnp
from jax import lax
from jax.experimental import pallas as pl
from jax.experimental.pallas import tpu as pltpu
from jax.sharding import Mesh
from jax.sharding import PartitionSpec as P

HEADS = 8
EPS = 1e-06
AXES = ("yh", "yl", "x", "zh", "zl", "core")
F32 = jnp.float32
BF16 = jnp.bfloat16


def dot(a, b, contract=((1,), (0,))):
    return lax.dot_general(a, b, (contract, ((), ())), preferred_element_type=F32)


def sigmoid(values):
    return 0.5 * jnp.tanh(0.5 * values) + 0.5


def normalised(values):
    average = jnp.mean(values, axis=-1, keepdims=True)
    centered = values - average
    spread = jnp.mean(centered * centered, axis=-1, keepdims=True)
    scale = lax.rsqrt(spread + EPS)
    return centered * scale, scale


def norm_backward(grad, normed, scale):
    first = jnp.mean(grad, axis=-1, keepdims=True)
    second = jnp.mean(grad * normed, axis=-1, keepdims=True)
    return scale * (grad - first - normed * second)


def weight_kernel(
    length_ref,
    hist_ref,
    cot_ref,
    win_ref,
    wout_ref,
    tiles_ref,
    dpre_ref,
    normed_ref,
    turned_ref,
    seed_ref,
    proj_ref,
    slope_ref,
    mixed_ref,
    dgated_ref,
):
    slots, positions, features = hist_ref.shape
    pairs = features // 128
    rows = slots * positions
    half = positions

    def prepare(i, carry):
        at = pl.ds(pl.multiple_of(i * positions, positions), positions)
        normed, _ = normalised(hist_ref[i].astype(F32))
        normed_ref[at, :] = normed.astype(BF16)
        row = lax.broadcasted_iota(jnp.int32, (positions, features), 0)
        cot = cot_ref[i].astype(F32)
        seed_ref[at, :] = jnp.where(row < length_ref[i], cot, 0.0).astype(BF16)
        return carry

    lax.fori_loop(0, slots, prepare, 0)
    turned_ref[...] = normed_ref[...].T

    width = 256
    for j in range(4 * features // width):
        columns = slice(j * width, (j + 1) * width)
        pre = dot(normed_ref[...], win_ref[:, columns])
        gate = sigmoid(pre)
        value = pre * gate
        proj_ref[:, columns] = value.astype(BF16)
        slope_ref[:, columns] = gate + value * (1.0 - gate)
    dgated_ref[...] = dot(seed_ref[...], wout_ref[...], ((1,), (1,))).astype(BF16)

    lane = lax.broadcasted_iota(jnp.int32, (positions, 128), 1)
    time = lax.broadcasted_iota(jnp.int32, (positions, 128), 0)
    first = lane < half
    source = jnp.where(first, lane, lane - half)
    causal = source <= time

    def spread(block):
        zero = jnp.zeros_like(block)
        return jnp.concatenate([jnp.where(first, block, zero), jnp.where(first, zero, block)], 0)

    def attend(i, carry):
        at = pl.ds(pl.multiple_of(i * positions, positions), positions)
        length = length_ref[i]
        inverse = 1.0 / jnp.maximum(length, 1).astype(F32)
        allowed = causal & (source < length)
        weights, slopes = [], []
        for p in range(pairs):
            v_at = slice(features + p * 128, features + (p + 1) * 128)
            q_at = slice(2 * features + p * 128, 2 * features + (p + 1) * 128)
            k_at = slice(3 * features + p * 128, 3 * features + (p + 1) * 128)
            scores = dot(proj_ref[at, q_at], spread(proj_ref[at, k_at]), ((1,), (1,))) * 0.125
            gate = sigmoid(scores)
            value = scores * gate
            weights.append(jnp.where(allowed, value * inverse, 0.0).astype(BF16))
            slopes.append(
                jnp.where(allowed, (gate + value * (1.0 - gate)) * (inverse * 0.125), 0.0)
            )
            mixed_ref[:, p * 128 : (p + 1) * 128] = dot(weights[p], spread(proj_ref[at, v_at]))
        normed, scale = normalised(mixed_ref[...])
        dgated = dgated_ref[at, :].astype(F32)
        dgate = dgated * normed
        dpre_ref[at, :features] = (dgate * slope_ref[at, :features]).astype(BF16)
        dmixed = norm_backward(dgated * proj_ref[at, :features].astype(F32), normed, scale)
        dmixed = dmixed.astype(BF16)
        for p in range(pairs):
            v_at = slice(features + p * 128, features + (p + 1) * 128)
            q_at = slice(2 * features + p * 128, 2 * features + (p + 1) * 128)
            k_at = slice(3 * features + p * 128, 3 * features + (p + 1) * 128)
            down = dmixed[:, p * 128 : (p + 1) * 128]
            dweights = dot(down, spread(proj_ref[at, v_at]), ((1,), (1,)))
            dscores = (dweights * slopes[p]).astype(BF16)
            dv = dot(weights[p], down, ((0,), (0,)))
            dv = jnp.where(first, dv[:half], dv[half:])
            dq = dot(dscores, spread(proj_ref[at, k_at]))
            dk = dot(dscores, proj_ref[at, q_at], ((0,), (0,)))
            dk = jnp.where(first, dk[:half], dk[half:])
            dpre_ref[at, v_at] = (dv * slope_ref[at, v_at]).astype(BF16)
            dpre_ref[at, q_at] = (dq * slope_ref[at, q_at]).astype(BF16)
            dpre_ref[at, k_at] = (dk * slope_ref[at, k_at]).astype(BF16)
        return carry

    lax.fori_loop(0, slots, attend, 0)

    left = lax.broadcasted_iota(jnp.int32, (16, 128), 1) < 64
    for y in range(8):
        block = dot(turned_ref[...], dpre_ref[:, y * 256 : (y + 1) * 256])
        for pair in range(2):
            part = block[:, pair * 128 : (pair + 1) * 128]
            swapped = pltpu.roll(part, 64, 1)
            for r in range(16):
                upper = slice(r * 32, r * 32 + 16)
                lower = slice(r * 32 + 16, r * 32 + 32)
                z, core = r // 2, r % 2
                even = jnp.where(left, part[upper], swapped[lower])
                odd = jnp.where(left, swapped[upper], part[lower])
                for x, tile in ((2 * pair, even), (2 * pair + 1, odd)):
                    q = x * 4 + (y % 2) * 2 + z % 2
                    place = q * 16 + (y // 2) * 4 + z // 2
                    tiles_ref[core, place] = tile.astype(BF16)


def history_kernel(length_ref, hist_ref, cot_ref, win_ref, dpre_ref, out_ref):
    slots, positions, features = hist_ref.shape

    def finish(i, carry):
        at = pl.ds(pl.multiple_of(i * positions, positions), positions)
        grad = dot(dpre_ref[at, :], win_ref[...], ((1,), (1,)))
        normed, scale = normalised(hist_ref[i].astype(F32))
        row = lax.broadcasted_iota(jnp.int32, (positions, features), 0)
        seed = jnp.where(row < length_ref[i], cot_ref[i].astype(F32), 0.0)
        out_ref[i] = (seed + norm_backward(grad, normed, scale)).astype(BF16)
        return carry

    lax.fori_loop(0, slots, finish, 0)


VMEM = pl.BlockSpec(memory_space=pltpu.VMEM)
SMEM = pl.BlockSpec(memory_space=pltpu.SMEM)


def weight_tiles(lengths, hist, cot, w_in, w_out):
    slots, positions, features = hist.shape
    rows = slots * positions
    return pl.pallas_call(
        weight_kernel,
        out_shape=(
            jax.ShapeDtypeStruct((2, 256, 16, 128), BF16),
            jax.ShapeDtypeStruct((rows, 4 * features), BF16),
        ),
        in_specs=[SMEM, VMEM, VMEM, VMEM, VMEM],
        out_specs=(VMEM, VMEM),
        scratch_shapes=[
            pltpu.VMEM((rows, features), BF16),
            pltpu.VMEM((features, rows), BF16),
            pltpu.VMEM((rows, features), BF16),
            pltpu.VMEM((rows, 4 * features), BF16),
            pltpu.VMEM((rows, 4 * features), F32),
            pltpu.VMEM((positions, features), F32),
            pltpu.VMEM((rows, features), BF16),
        ],
        compiler_params=pltpu.CompilerParams(vmem_limit_bytes=40 * 2**20),
        cost_estimate=pl.CostEstimate(
            flops=2 * rows * features * features * 9, bytes_accessed=8 * 2**20, transcendentals=10**6
        ),
    )(lengths, hist, cot, w_in, w_out)


def history_grads(lengths, hist, cot, w_in, dpre):
    return pl.pallas_call(
        history_kernel,
        out_shape=jax.ShapeDtypeStruct(hist.shape, BF16),
        in_specs=[SMEM, VMEM, VMEM, VMEM, VMEM],
        out_specs=VMEM,
        compiler_params=pltpu.CompilerParams(vmem_limit_bytes=24 * 2**20),
        cost_estimate=pl.CostEstimate(
            flops=2 * dpre.shape[0] * dpre.shape[1] * hist.shape[-1],
            bytes_accessed=6 * 2**20,
            transcendentals=1000,
        ),
    )(lengths, hist, cot, w_in, dpre)


STEPS = (("x", "yl", "zl"), ("yh", "zh"))


def summed(parts):
    return jnp.sum(parts.astype(F32), axis=0)


def reduced(tiles):
    tiles = lax.all_to_all(tiles, "core", 0, 0, tiled=True)
    for axes in STEPS:
        tiles = summed(tiles).astype(BF16)
        tiles = tiles.reshape(16, -1, *tiles.shape[1:])
        tiles = lax.all_to_all(tiles, axes, 0, 0, tiled=True)
    return summed(tiles)[0]


def shards(histories, cotangents, lengths, w_in, w_out):
    hist, cot, slot_lengths = histories[0, 0], cotangents[0, 0], lengths[0, 0]
    tiles, dpre = weight_tiles(slot_lengths, hist, cot, w_in, w_out)
    grads = history_grads(slot_lengths, hist, cot, w_in, dpre)
    tile = reduced(tiles)
    block = jnp.concatenate([tile[:, :64], tile[:, 64:]], axis=0)
    return (grads[None, None], block)


def solution(mesh):
    torus = Mesh(mesh.devices.reshape(4, 2, 4, 4, 2, 2), AXES)
    seq, rep = ("yh", "yl", "x"), ("zh", "zl", "core")
    placed = (
        P(rep, seq, None, None, None),
        P(rep, seq, None, None, None),
        P(rep, seq, None),
        P(),
        P(),
    )
    return jax.shard_map(
        shards,
        mesh=torus,
        in_specs=placed,
        out_specs=(P(rep, seq, None, None, None), P(rep, seq)),
        check_vma=False,
    )
```

```python
import jax
import jax.numpy as jnp
from jax import lax
from jax.experimental import pallas as pl
from jax.experimental.pallas import tpu as pltpu
from jax.sharding import Mesh
from jax.sharding import PartitionSpec as P

HEADS = 8
EPS = 1e-06
AXES = ("yh", "yl", "x", "zh", "zl", "core")
F32 = jnp.float32
BF16 = jnp.bfloat16


def dot(a, b, contract=((1,), (0,))):
    return lax.dot_general(a, b, (contract, ((), ())), preferred_element_type=F32)


def sigmoid(values):
    return 0.5 * jnp.tanh(0.5 * values) + 0.5


def normalised(values):
    average = jnp.mean(values, axis=-1, keepdims=True)
    centered = values - average
    spread = jnp.mean(centered * centered, axis=-1, keepdims=True)
    scale = lax.rsqrt(spread + EPS)
    return centered * scale, scale


def norm_backward(grad, normed, scale):
    first = jnp.mean(grad, axis=-1, keepdims=True)
    second = jnp.mean(grad * normed, axis=-1, keepdims=True)
    return scale * (grad - first - normed * second)


def weight_kernel(
    length_ref,
    hist_hbm,
    cot_hbm,
    win_hbm,
    wout_hbm,
    tiles_hbm,
    dpre_hbm,
    done_ref,
    tiles_ref,
    dpre_ref,
    hist_ref,
    cot_ref,
    win_ref,
    wout_ref,
    normed_ref,
    turned_ref,
    seed_ref,
    proj_ref,
    slope_ref,
    mixed_ref,
    dgated_ref,
    arrived,
    sent,
):
    slots, positions, features = hist_ref.shape
    pairs = features // 128
    half = positions

    def columns_of(ref, j):
        return ref.at[:, j * features : (j + 1) * features]

    hist_copy = pltpu.make_async_copy(hist_hbm, hist_ref, arrived.at[0])
    win_copies = [
        pltpu.make_async_copy(columns_of(win_hbm, j), columns_of(win_ref, j), arrived.at[1 + j])
        for j in range(4)
    ]
    cot_copy = pltpu.make_async_copy(cot_hbm, cot_ref, arrived.at[5])
    wout_copy = pltpu.make_async_copy(wout_hbm, wout_ref, arrived.at[6])
    for copy in (hist_copy, *win_copies, cot_copy, wout_copy):
        copy.start()

    done_ref[...] = jnp.zeros_like(done_ref)
    hist_copy.wait()

    def prepare(i, carry):
        at = pl.ds(pl.multiple_of(i * positions, positions), positions)
        normed, _ = normalised(hist_ref[i].astype(F32))
        normed_ref[at, :] = normed.astype(BF16)
        return carry

    lax.fori_loop(0, slots, prepare, 0)
    turned_ref[...] = normed_ref[...].T

    width = 256
    for j in range(4 * features // width):
        if (j * width) % features == 0:
            win_copies[j * width // features].wait()
        columns = slice(j * width, (j + 1) * width)
        pre = dot(normed_ref[...], win_ref[:, columns])
        gate = sigmoid(pre)
        value = pre * gate
        proj_ref[:, columns] = value.astype(BF16)
        slope_ref[:, columns] = gate + value * (1.0 - gate)
    cot_copy.wait()

    def mask(i, carry):
        at = pl.ds(pl.multiple_of(i * positions, positions), positions)
        row = lax.broadcasted_iota(jnp.int32, (positions, features), 0)
        cot = cot_ref[i].astype(F32)
        seed_ref[at, :] = jnp.where(row < length_ref[i], cot, 0.0).astype(BF16)
        return carry

    lax.fori_loop(0, slots, mask, 0)
    wout_copy.wait()
    dgated_ref[...] = dot(seed_ref[...], wout_ref[...], ((1,), (1,))).astype(BF16)

    lane = lax.broadcasted_iota(jnp.int32, (positions, 128), 1)
    time = lax.broadcasted_iota(jnp.int32, (positions, 128), 0)
    first = lane < half
    source = jnp.where(first, lane, lane - half)
    causal = source <= time

    def spread(block):
        zero = jnp.zeros_like(block)
        return jnp.concatenate([jnp.where(first, block, zero), jnp.where(first, zero, block)], 0)

    def attend(i, carry):
        at = pl.ds(pl.multiple_of(i * positions, positions), positions)
        length = length_ref[i]
        inverse = 1.0 / jnp.maximum(length, 1).astype(F32)
        allowed = causal & (source < length)
        weights, slopes = [], []
        for p in range(pairs):
            v_at = slice(features + p * 128, features + (p + 1) * 128)
            q_at = slice(2 * features + p * 128, 2 * features + (p + 1) * 128)
            k_at = slice(3 * features + p * 128, 3 * features + (p + 1) * 128)
            scores = dot(proj_ref[at, q_at], spread(proj_ref[at, k_at]), ((1,), (1,))) * 0.125
            gate = sigmoid(scores)
            value = scores * gate
            weights.append(jnp.where(allowed, value * inverse, 0.0).astype(BF16))
            slopes.append(
                jnp.where(allowed, (gate + value * (1.0 - gate)) * (inverse * 0.125), 0.0)
            )
            mixed_ref[:, p * 128 : (p + 1) * 128] = dot(weights[p], spread(proj_ref[at, v_at]))
        normed, scale = normalised(mixed_ref[...])
        dgated = dgated_ref[at, :].astype(F32)
        dgate = dgated * normed
        dpre_ref[at, :features] = (dgate * slope_ref[at, :features]).astype(BF16)
        dmixed = norm_backward(dgated * proj_ref[at, :features].astype(F32), normed, scale)
        dmixed = dmixed.astype(BF16)
        for p in range(pairs):
            v_at = slice(features + p * 128, features + (p + 1) * 128)
            q_at = slice(2 * features + p * 128, 2 * features + (p + 1) * 128)
            k_at = slice(3 * features + p * 128, 3 * features + (p + 1) * 128)
            down = dmixed[:, p * 128 : (p + 1) * 128]
            dweights = dot(down, spread(proj_ref[at, v_at]), ((1,), (1,)))
            dscores = (dweights * slopes[p]).astype(BF16)
            dv = dot(weights[p], down, ((0,), (0,)))
            dv = jnp.where(first, dv[:half], dv[half:])
            dq = dot(dscores, spread(proj_ref[at, k_at]))
            dk = dot(dscores, proj_ref[at, q_at], ((0,), (0,)))
            dk = jnp.where(first, dk[:half], dk[half:])
            dpre_ref[at, v_at] = (dv * slope_ref[at, v_at]).astype(BF16)
            dpre_ref[at, q_at] = (dq * slope_ref[at, q_at]).astype(BF16)
            dpre_ref[at, k_at] = (dk * slope_ref[at, k_at]).astype(BF16)
        return carry

    lax.fori_loop(0, slots, attend, 0)

    dpre_copy = pltpu.make_async_copy(dpre_ref, dpre_hbm, sent.at[8])
    dpre_copy.start()
    tile_copies = []
    left = lax.broadcasted_iota(jnp.int32, (16, 128), 1) < 64
    for y in range(8):
        block = dot(turned_ref[...], dpre_ref[:, y * 256 : (y + 1) * 256])
        for pair in range(2):
            part = block[:, pair * 128 : (pair + 1) * 128]
            swapped = pltpu.roll(part, 64, 1)
            for r in range(16):
                upper = slice(r * 32, r * 32 + 16)
                lower = slice(r * 32 + 16, r * 32 + 32)
                z, core = r // 2, r % 2
                even = jnp.where(left, part[upper], swapped[lower])
                odd = jnp.where(left, swapped[upper], part[lower])
                for x, tile in ((2 * pair, even), (2 * pair + 1, odd)):
                    place = (x, y % 2, z % 2, y // 2, z // 2)
                    tiles_ref[(core, *place)] = tile.astype(BF16)
        part = (slice(None), slice(None), y % 2, slice(None), y // 2)
        tile_copies.append(
            pltpu.make_async_copy(tiles_ref.at[part], tiles_hbm.at[part], sent.at[y])
        )
        tile_copies[y].start()
    for copy in (dpre_copy, *tile_copies):
        copy.wait()


def history_kernel(
    length_ref, hist_ref, cot_ref, win_ref, dpre_ref, after_ref, out_ref, done_ref, grad_ref
):
    slots, positions, features = hist_ref.shape
    grad_ref[...] = dot(dpre_ref[...], win_ref[...], ((1,), (1,)))

    def finish(i, carry):
        at = pl.ds(pl.multiple_of(i * positions, positions), positions)
        normed, scale = normalised(hist_ref[i].astype(F32))
        row = lax.broadcasted_iota(jnp.int32, (positions, features), 0)
        seed = jnp.where(row < length_ref[i], cot_ref[i].astype(F32), 0.0)
        out_ref[i] = (seed + norm_backward(grad_ref[at, :], normed, scale)).astype(BF16)
        return carry

    lax.fori_loop(0, slots, finish, 0)
    done_ref[...] = jnp.zeros_like(done_ref)


def sum_kernel(parts_ref, after_ref, out_ref, done_ref):
    parts, count = parts_ref.shape[:2]
    step = min(count, 8)

    def add(i, carry):
        at = pl.ds(i * step, step)
        total = parts_ref[0, at].astype(F32)
        for p in range(1, parts):
            total += parts_ref[p, at].astype(F32)
        out_ref[at] = total.astype(BF16)
        return carry

    lax.fori_loop(0, count // step, add, 0)
    done_ref[...] = jnp.zeros_like(done_ref)


def last_kernel(parts_ref, out_ref):
    total = parts_ref[0, 0].astype(F32)
    for p in range(1, parts_ref.shape[0]):
        total += parts_ref[p, 0].astype(F32)
    out_ref[:16, :] = total[:, :64]
    out_ref[16:, :] = total[:, 64:]


VMEM = pl.BlockSpec(memory_space=pltpu.VMEM)
SMEM = pl.BlockSpec(memory_space=pltpu.SMEM)
HBM = pl.BlockSpec(memory_space=pltpu.HBM)
TILES = (2, 4, 2, 2, 4, 4, 16, 128)
DONE = jax.ShapeDtypeStruct((8, 128), F32)


def weight_tiles(lengths, hist, cot, w_in, w_out):
    slots, positions, features = hist.shape
    rows = slots * positions
    return pl.pallas_call(
        weight_kernel,
        out_shape=(
            jax.ShapeDtypeStruct(TILES, BF16),
            jax.ShapeDtypeStruct((rows, 4 * features), BF16),
            DONE,
        ),
        in_specs=[SMEM, HBM, HBM, HBM, HBM],
        out_specs=(HBM, HBM, VMEM),
        scratch_shapes=[
            pltpu.VMEM(TILES, BF16),
            pltpu.VMEM((rows, 4 * features), BF16),
            pltpu.VMEM(hist.shape, BF16),
            pltpu.VMEM(hist.shape, BF16),
            pltpu.VMEM(w_in.shape, BF16),
            pltpu.VMEM(w_out.shape, BF16),
            pltpu.VMEM((rows, features), BF16),
            pltpu.VMEM((features, rows), BF16),
            pltpu.VMEM((rows, features), BF16),
            pltpu.VMEM((rows, 4 * features), BF16),
            pltpu.VMEM((rows, 4 * features), F32),
            pltpu.VMEM((positions, features), F32),
            pltpu.VMEM((rows, features), BF16),
            pltpu.SemaphoreType.DMA((7,)),
            pltpu.SemaphoreType.DMA((9,)),
        ],
        compiler_params=pltpu.CompilerParams(vmem_limit_bytes=56 * 2**20),
        cost_estimate=pl.CostEstimate(
            flops=2 * rows * features * features * 9, bytes_accessed=8 * 2**20, transcendentals=10**6
        ),
    )(lengths, hist, cot, w_in, w_out)


def history_grads(lengths, hist, cot, w_in, dpre, after):
    rows = dpre.shape[0]
    return pl.pallas_call(
        history_kernel,
        out_shape=(jax.ShapeDtypeStruct(hist.shape, BF16), DONE),
        in_specs=[SMEM, VMEM, VMEM, VMEM, VMEM, VMEM],
        out_specs=(VMEM, VMEM),
        scratch_shapes=[pltpu.VMEM((rows, hist.shape[-1]), F32)],
        compiler_params=pltpu.CompilerParams(vmem_limit_bytes=16 * 2**20),
        cost_estimate=pl.CostEstimate(
            flops=2 * rows * dpre.shape[1] * hist.shape[-1],
            bytes_accessed=6 * 2**20,
            transcendentals=1000,
        ),
    )(lengths, hist, cot, w_in, dpre, after)


def summed(parts, after):
    return pl.pallas_call(
        sum_kernel,
        out_shape=(jax.ShapeDtypeStruct(parts.shape[1:], BF16), DONE),
        in_specs=[VMEM, VMEM],
        out_specs=(VMEM, VMEM),
        compiler_params=pltpu.CompilerParams(vmem_limit_bytes=8 * 2**20),
    )(parts, after)


def last_sum(parts):
    return pl.pallas_call(
        last_kernel,
        out_shape=jax.ShapeDtypeStruct((32, 64), F32),
        in_specs=[VMEM],
        out_specs=VMEM,
        compiler_params=pltpu.CompilerParams(vmem_limit_bytes=2 * 2**20),
    )(parts)


def exchanged(tiles, axes):
    return lax.all_to_all(tiles, axes, 0, 0, tiled=True)


def shards(histories, cotangents, lengths, w_in, w_out):
    hist, cot, slot_lengths = histories[0, 0], cotangents[0, 0], lengths[0, 0]
    tiles, dpre, done = weight_tiles(slot_lengths, hist, cot, w_in, w_out)
    tiles, done = summed(exchanged(tiles.reshape(2, 256, 16, 128), "core"), done)
    near = exchanged(tiles.reshape(16, 16, 16, 128), ("x", "yl", "zl"))
    grads, done = history_grads(slot_lengths, hist, cot, w_in, dpre, done)
    tiles, done = summed(near, done)
    block = last_sum(exchanged(tiles.reshape(16, 1, 16, 128), ("yh", "zh")))
    return (grads[None, None], block)


def solution(mesh):
    torus = Mesh(mesh.devices.reshape(4, 2, 4, 4, 2, 2), AXES)
    seq, rep = ("yh", "yl", "x"), ("zh", "zl", "core")
    placed = (
        P(rep, seq, None, None, None),
        P(rep, seq, None, None, None),
        P(rep, seq, None),
        P(),
        P(),
    )
    return jax.shard_map(
        shards,
        mesh=torus,
        in_specs=placed,
        out_specs=(P(rep, seq, None, None, None), P(rep, seq)),
        check_vma=False,
    )
```

```python
import jax
import jax.numpy as jnp
from jax import lax
from jax.experimental import pallas as pl
from jax.experimental.pallas import tpu as pltpu
from jax.sharding import Mesh
from jax.sharding import PartitionSpec as P

HEADS = 8
EPS = 1e-06
UNROLL = 6
AXES = ("yh", "yl", "x", "zh", "zl", "core")
F32 = jnp.float32
BF16 = jnp.bfloat16


def dot(a, b, contract=((1,), (0,))):
    return lax.dot_general(a, b, (contract, ((), ())), preferred_element_type=F32)


def sigmoid(values):
    return 0.5 * jnp.tanh(0.5 * values) + 0.5


def normalised(values):
    average = jnp.mean(values, axis=-1, keepdims=True)
    centered = values - average
    spread = jnp.mean(centered * centered, axis=-1, keepdims=True)
    scale = lax.rsqrt(spread + EPS)
    return centered * scale, scale


def norm_backward(grad, normed, scale):
    first = jnp.mean(grad, axis=-1, keepdims=True)
    second = jnp.mean(grad * normed, axis=-1, keepdims=True)
    return scale * (grad - first - normed * second)


def weight_kernel(
    length_ref,
    hist_hbm,
    cot_hbm,
    win_hbm,
    wout_hbm,
    keep_hbm,
    send_hbm,
    dpre_hbm,
    tiles_ref,
    dpre_ref,
    hist_ref,
    cot_ref,
    win_ref,
    wout_ref,
    normed_ref,
    turned_ref,
    seed_ref,
    proj_ref,
    slope_ref,
    mixed_ref,
    dgated_ref,
    scores_ref,
    weights_ref,
    dmixed_ref,
    dscores_ref,
    arrived,
    sent,
):
    slots, positions, features = hist_ref.shape
    pairs = features // 128
    half = positions

    def columns_of(ref, j):
        return ref.at[:, j * features : (j + 1) * features]

    hist_copy = pltpu.make_async_copy(hist_hbm, hist_ref, arrived.at[0])
    win_copies = [
        pltpu.make_async_copy(columns_of(win_hbm, j), columns_of(win_ref, j), arrived.at[1 + j])
        for j in range(4)
    ]
    cot_copy = pltpu.make_async_copy(cot_hbm, cot_ref, arrived.at[5])
    wout_copy = pltpu.make_async_copy(wout_hbm, wout_ref, arrived.at[6])
    for copy in (hist_copy, *win_copies, cot_copy, wout_copy):
        copy.start()

    hist_copy.wait()

    def prepare(i, carry):
        at = pl.ds(pl.multiple_of(i * positions, positions), positions)
        normed, _ = normalised(hist_ref[i].astype(F32))
        normed_ref[at, :] = normed.astype(BF16)
        return carry

    lax.fori_loop(0, slots, prepare, 0, unroll=UNROLL)
    turned_ref[...] = normed_ref[...].T

    width = 256
    for j in range(4 * features // width):
        if (j * width) % features == 0:
            win_copies[j * width // features].wait()
        columns = slice(j * width, (j + 1) * width)
        pre = dot(normed_ref[...], win_ref[:, columns])
        gate = sigmoid(pre)
        value = pre * gate
        proj_ref[:, columns] = value.astype(BF16)
        slope_ref[:, columns] = gate + value * (1.0 - gate)
    cot_copy.wait()

    def mask(i, carry):
        at = pl.ds(pl.multiple_of(i * positions, positions), positions)
        row = lax.broadcasted_iota(jnp.int32, (positions, features), 0)
        cot = cot_ref[i].astype(F32)
        seed_ref[at, :] = jnp.where(row < length_ref[i], cot, 0.0).astype(BF16)
        return carry

    lax.fori_loop(0, slots, mask, 0, unroll=UNROLL)
    wout_copy.wait()
    dgated_ref[...] = dot(seed_ref[...], wout_ref[...], ((1,), (1,))).astype(BF16)

    lane = lax.broadcasted_iota(jnp.int32, (positions, 128), 1)
    first = lane < half
    early = jnp.where(first, 1.0, 0.0).astype(BF16)
    late = jnp.where(first, 0.0, 1.0).astype(BF16)

    def spread(block):
        return jnp.concatenate([block * early, block * late], 0)

    def blocks(p):
        return [slice(b * features + p * 128, b * features + (p + 1) * 128) for b in range(4)]

    def for_slots(body):
        def step(i, carry):
            body(i, pl.ds(pl.multiple_of(i * positions, positions), positions))
            return carry

        lax.fori_loop(0, slots, step, 0, unroll=UNROLL)

    def score(i, at):
        for p in range(pairs):
            _, _, q_at, k_at = blocks(p)
            scores_ref[at, blocks(p)[0]] = dot(
                proj_ref[at, q_at], spread(proj_ref[at, k_at]), ((1,), (1,))
            )

    def weigh(i, at):
        length = length_ref[i]
        inverse = 1.0 / jnp.maximum(length, 1).astype(F32)
        source = lax.broadcasted_iota(jnp.int32, (positions, features), 1) % half
        time = lax.broadcasted_iota(jnp.int32, (positions, features), 0)
        allowed = (source <= time) & (source < length)
        scores = scores_ref[at, :] * 0.125
        gate = sigmoid(scores)
        value = scores * gate
        weights_ref[at, :] = jnp.where(allowed, value * inverse, 0.0).astype(BF16)
        slopes = (gate + value * (1.0 - gate)) * (inverse * 0.125)
        scores_ref[at, :] = jnp.where(allowed, slopes, 0.0)

    def mix(i, at):
        for p in range(pairs):
            here, v_at, _, _ = blocks(p)
            mixed_ref[at, here] = dot(weights_ref[at, here], spread(proj_ref[at, v_at]))

    def turn(i, at):
        normed, scale = normalised(mixed_ref[at, :])
        dgated = dgated_ref[at, :].astype(F32)
        dpre_ref[at, :features] = (dgated * normed * slope_ref[at, :features]).astype(BF16)
        dmixed = norm_backward(dgated * proj_ref[at, :features].astype(F32), normed, scale)
        dmixed_ref[at, :] = dmixed.astype(BF16)

    def value_back(i, at):
        for p in range(pairs):
            here, v_at, _, _ = blocks(p)
            down = dmixed_ref[at, here]
            dweights = dot(down, spread(proj_ref[at, v_at]), ((1,), (1,)))
            dscores_ref[at, here] = (dweights * scores_ref[at, here]).astype(BF16)
            dv = dot(weights_ref[at, here], down, ((0,), (0,)))
            dv = jnp.where(first, dv[:half], dv[half:])
            dpre_ref[at, v_at] = (dv * slope_ref[at, v_at]).astype(BF16)

    def score_back(i, at):
        for p in range(pairs):
            here, _, q_at, k_at = blocks(p)
            dq = dot(dscores_ref[at, here], spread(proj_ref[at, k_at]))
            dk = dot(dscores_ref[at, here], proj_ref[at, q_at], ((0,), (0,)))
            dk = jnp.where(first, dk[:half], dk[half:])
            dpre_ref[at, q_at] = (dq * slope_ref[at, q_at]).astype(BF16)
            dpre_ref[at, k_at] = (dk * slope_ref[at, k_at]).astype(BF16)

    for body in (score, weigh, mix, turn, value_back, score_back):
        for_slots(body)

    dpre_copy = pltpu.make_async_copy(dpre_ref, dpre_hbm, sent.at[64])
    dpre_copy.start()
    tile_copies = []
    core = lax.axis_index("core")
    left = lax.broadcasted_iota(jnp.int32, (16, 128), 1) < 64
    for y in range(8):
        block = dot(turned_ref[...], dpre_ref[:, y * 256 : (y + 1) * 256])
        for pair in range(2):
            part = block[:, pair * 128 : (pair + 1) * 128]
            swapped = pltpu.roll(part, 64, 1)
            for r in range(16):
                upper = slice(r * 32, r * 32 + 16)
                lower = slice(r * 32 + 16, r * 32 + 32)
                z = r // 2
                even = jnp.where(left, part[upper], swapped[lower])
                odd = jnp.where(left, swapped[upper], part[lower])
                for x, tile in ((2 * pair, even), (2 * pair + 1, odd)):
                    place = (x, y % 2, z % 2, y // 2, z // 2)
                    tiles_ref[(r % 2, *place)] = tile.astype(BF16)
        for x in range(4):
            for side, out_hbm in ((core, keep_hbm), (1 - core, send_hbm)):
                part = (x, y % 2, slice(None), y // 2)
                copy = pltpu.make_async_copy(
                    tiles_ref.at[(side, *part)], out_hbm.at[part], sent.at[len(tile_copies)]
                )
                copy.start()
                tile_copies.append(copy)
    for copy in (dpre_copy, *tile_copies):
        copy.wait()


def history_kernel(
    length_ref, hist_ref, cot_ref, win_ref, dpre_ref, after_ref, out_ref, grad_ref
):
    slots, positions, features = hist_ref.shape
    grad_ref[...] = dot(dpre_ref[...], win_ref[...], ((1,), (1,)))

    def finish(i, carry):
        at = pl.ds(pl.multiple_of(i * positions, positions), positions)
        normed, scale = normalised(hist_ref[i].astype(F32))
        row = lax.broadcasted_iota(jnp.int32, (positions, features), 0)
        seed = jnp.where(row < length_ref[i], cot_ref[i].astype(F32), 0.0)
        out_ref[i] = (seed + norm_backward(grad_ref[at, :], normed, scale)).astype(BF16)
        return carry

    lax.fori_loop(0, slots, finish, 0, unroll=UNROLL)


def pair_kernel(one_ref, other_ref, out_ref):
    step = 16

    def add(i, carry):
        at = pl.ds(i * step, step)
        out_ref[at] = (one_ref[at].astype(F32) + other_ref[at].astype(F32)).astype(BF16)
        return carry

    lax.fori_loop(0, out_ref.shape[0] // step, add, 0)


def sum_kernel(parts_ref, out_ref, done_ref):
    parts, count = parts_ref.shape[:2]
    step = 4

    def add(i, carry):
        at = pl.ds(i * step, step)
        total = parts_ref[0, at].astype(F32)
        for p in range(1, parts):
            total += parts_ref[p, at].astype(F32)
        out_ref[at] = total.astype(BF16)
        return carry

    lax.fori_loop(0, count // step, add, 0)
    done_ref[...] = jnp.zeros_like(done_ref)


def last_kernel(parts_ref, out_ref):
    total = parts_ref[0, 0].astype(F32)
    for p in range(1, parts_ref.shape[0]):
        total += parts_ref[p, 0].astype(F32)
    out_ref[:16, :] = total[:, :64]
    out_ref[16:, :] = total[:, 64:]


VMEM = pl.BlockSpec(memory_space=pltpu.VMEM)
SMEM = pl.BlockSpec(memory_space=pltpu.SMEM)
HBM = pl.BlockSpec(memory_space=pltpu.HBM)
TILES = (4, 2, 2, 4, 4, 16, 128)
DONE = jax.ShapeDtypeStruct((8, 128), F32)


def weight_tiles(lengths, hist, cot, w_in, w_out):
    slots, positions, features = hist.shape
    rows = slots * positions
    return pl.pallas_call(
        weight_kernel,
        out_shape=(
            jax.ShapeDtypeStruct(TILES, BF16),
            jax.ShapeDtypeStruct(TILES, BF16),
            jax.ShapeDtypeStruct((rows, 4 * features), BF16),
        ),
        in_specs=[SMEM, HBM, HBM, HBM, HBM],
        out_specs=(HBM, HBM, HBM),
        scratch_shapes=[
            pltpu.VMEM((2, *TILES), BF16),
            pltpu.VMEM((rows, 4 * features), BF16),
            pltpu.VMEM(hist.shape, BF16),
            pltpu.VMEM(hist.shape, BF16),
            pltpu.VMEM(w_in.shape, BF16),
            pltpu.VMEM(w_out.shape, BF16),
            pltpu.VMEM((rows, features), BF16),
            pltpu.VMEM((features, rows), BF16),
            pltpu.VMEM((rows, features), BF16),
            pltpu.VMEM((rows, 4 * features), BF16),
            pltpu.VMEM((rows, 4 * features), F32),
            pltpu.VMEM((rows, features), F32),
            pltpu.VMEM((rows, features), BF16),
            pltpu.VMEM((rows, features), F32),
            pltpu.VMEM((rows, features), BF16),
            pltpu.VMEM((rows, features), BF16),
            pltpu.VMEM((rows, features), BF16),
            pltpu.SemaphoreType.DMA((7,)),
            pltpu.SemaphoreType.DMA((65,)),
        ],
        compiler_params=pltpu.CompilerParams(vmem_limit_bytes=56 * 2**20),
        cost_estimate=pl.CostEstimate(
            flops=2 * rows * features * features * 9, bytes_accessed=8 * 2**20, transcendentals=10**6
        ),
    )(lengths, hist, cot, w_in, w_out)


def history_grads(lengths, hist, cot, w_in, dpre, after):
    rows = dpre.shape[0]
    return pl.pallas_call(
        history_kernel,
        out_shape=jax.ShapeDtypeStruct(hist.shape, BF16),
        in_specs=[SMEM, VMEM, VMEM, VMEM, VMEM, VMEM],
        out_specs=VMEM,
        scratch_shapes=[pltpu.VMEM((rows, hist.shape[-1]), F32)],
        compiler_params=pltpu.CompilerParams(vmem_limit_bytes=16 * 2**20),
        cost_estimate=pl.CostEstimate(
            flops=2 * rows * dpre.shape[1] * hist.shape[-1],
            bytes_accessed=6 * 2**20,
            transcendentals=1000,
        ),
    )(lengths, hist, cot, w_in, dpre, after)


def pair_sum(one, other):
    return pl.pallas_call(
        pair_kernel,
        out_shape=jax.ShapeDtypeStruct(one.shape, BF16),
        in_specs=[VMEM, VMEM],
        out_specs=VMEM,
        compiler_params=pltpu.CompilerParams(vmem_limit_bytes=8 * 2**20),
    )(one, other)


def summed(parts):
    return pl.pallas_call(
        sum_kernel,
        out_shape=(jax.ShapeDtypeStruct(parts.shape[1:], BF16), DONE),
        in_specs=[VMEM],
        out_specs=(VMEM, VMEM),
        compiler_params=pltpu.CompilerParams(vmem_limit_bytes=8 * 2**20),
    )(parts)


def last_sum(parts):
    return pl.pallas_call(
        last_kernel,
        out_shape=jax.ShapeDtypeStruct((32, 64), F32),
        in_specs=[VMEM],
        out_specs=VMEM,
        compiler_params=pltpu.CompilerParams(vmem_limit_bytes=2 * 2**20),
    )(parts)


def exchanged(tiles, axes):
    return lax.all_to_all(tiles, axes, 0, 0, tiled=True)


def shards(histories, cotangents, lengths, w_in, w_out):
    hist, cot, slot_lengths = histories[0, 0], cotangents[0, 0], lengths[0, 0]
    keep, send, dpre = weight_tiles(slot_lengths, hist, cot, w_in, w_out)
    other = lax.ppermute(send.reshape(256, 16, 128), "core", [(0, 1), (1, 0)])
    tiles = pair_sum(keep.reshape(256, 16, 128), other)
    tiles, done = summed(exchanged(tiles.reshape(16, 16, 16, 128), ("x", "yl", "zl")))
    grads = history_grads(slot_lengths, hist, cot, w_in, dpre, done)
    block = last_sum(exchanged(tiles.reshape(16, 1, 16, 128), ("yh", "zh")))
    return (grads[None, None], block)


def solution(mesh):
    torus = Mesh(mesh.devices.reshape(4, 2, 4, 4, 2, 2), AXES)
    seq, rep = ("yh", "yl", "x"), ("zh", "zl", "core")
    placed = (
        P(rep, seq, None, None, None),
        P(rep, seq, None, None, None),
        P(rep, seq, None),
        P(),
        P(),
    )
    return jax.shard_map(
        shards,
        mesh=torus,
        in_specs=placed,
        out_specs=(P(rep, seq, None, None, None), P(rep, seq)),
        check_vma=False,
    )
```

```python
import jax
import jax.numpy as jnp
from jax import lax
from jax.experimental import pallas as pl
from jax.experimental.pallas import tpu as pltpu
from jax.sharding import Mesh
from jax.sharding import PartitionSpec as P

HEADS = 8
EPS = 1e-06
UNROLL = 6
AXES = ("yh", "yl", "x", "zh", "zl", "core")
F32 = jnp.float32
BF16 = jnp.bfloat16


def dot(a, b, contract=((1,), (0,))):
    return lax.dot_general(a, b, (contract, ((), ())), preferred_element_type=F32)


def sigmoid(values):
    return 0.5 * jnp.tanh(0.5 * values) + 0.5


def normalised(values):
    average = jnp.mean(values, axis=-1, keepdims=True)
    centered = values - average
    spread = jnp.mean(centered * centered, axis=-1, keepdims=True)
    scale = lax.rsqrt(spread + EPS)
    return centered * scale, scale


def norm_backward(grad, normed, scale):
    first = jnp.mean(grad, axis=-1, keepdims=True)
    second = jnp.mean(grad * normed, axis=-1, keepdims=True)
    return scale * (grad - first - normed * second)


def weight_kernel(
    length_ref,
    hist_hbm,
    cot_hbm,
    win_hbm,
    wout_hbm,
    send_hbm,
    turned_hbm,
    dpre_hbm,
    tiles_ref,
    dpre_ref,
    hist_ref,
    cot_ref,
    win_ref,
    wout_ref,
    normed_ref,
    turned_ref,
    seed_ref,
    proj_ref,
    slope_ref,
    mixed_ref,
    dgated_ref,
    scores_ref,
    weights_ref,
    dmixed_ref,
    dscores_ref,
    arrived,
    sent,
):
    slots, positions, features = hist_ref.shape
    pairs = features // 128
    half = positions

    def columns_of(ref, j):
        return ref.at[:, j * features : (j + 1) * features]

    hist_copy = pltpu.make_async_copy(hist_hbm, hist_ref, arrived.at[0])
    win_copies = [
        pltpu.make_async_copy(columns_of(win_hbm, j), columns_of(win_ref, j), arrived.at[1 + j])
        for j in range(4)
    ]
    cot_copy = pltpu.make_async_copy(cot_hbm, cot_ref, arrived.at[5])
    wout_copy = pltpu.make_async_copy(wout_hbm, wout_ref, arrived.at[6])
    for copy in (hist_copy, *win_copies, cot_copy, wout_copy):
        copy.start()

    hist_copy.wait()

    def prepare(i, carry):
        at = pl.ds(pl.multiple_of(i * positions, positions), positions)
        normed, _ = normalised(hist_ref[i].astype(F32))
        normed_ref[at, :] = normed.astype(BF16)
        return carry

    lax.fori_loop(0, slots, prepare, 0, unroll=UNROLL)
    turned = normed_ref[...].T
    for r in range(16):
        place = (r % 2) * 8 + r // 2
        turned_ref[place * 32 : (place + 1) * 32, :] = turned[r * 32 : (r + 1) * 32, :]
    turned_copy = pltpu.make_async_copy(turned_ref, turned_hbm, sent.at[33])
    turned_copy.start()

    width = 256
    for j in range(4 * features // width):
        if (j * width) % features == 0:
            win_copies[j * width // features].wait()
        columns = slice(j * width, (j + 1) * width)
        pre = dot(normed_ref[...], win_ref[:, columns])
        gate = sigmoid(pre)
        value = pre * gate
        proj_ref[:, columns] = value.astype(BF16)
        slope_ref[:, columns] = gate + value * (1.0 - gate)
    cot_copy.wait()

    def mask(i, carry):
        at = pl.ds(pl.multiple_of(i * positions, positions), positions)
        row = lax.broadcasted_iota(jnp.int32, (positions, features), 0)
        cot = cot_ref[i].astype(F32)
        seed_ref[at, :] = jnp.where(row < length_ref[i], cot, 0.0).astype(BF16)
        return carry

    lax.fori_loop(0, slots, mask, 0, unroll=UNROLL)
    wout_copy.wait()
    dgated_ref[...] = dot(seed_ref[...], wout_ref[...], ((1,), (1,))).astype(BF16)

    lane = lax.broadcasted_iota(jnp.int32, (positions, 128), 1)
    first = lane < half
    early = jnp.where(first, 1.0, 0.0).astype(BF16)
    late = jnp.where(first, 0.0, 1.0).astype(BF16)

    def spread(block):
        return jnp.concatenate([block * early, block * late], 0)

    def blocks(p):
        return [slice(b * features + p * 128, b * features + (p + 1) * 128) for b in range(4)]

    def for_slots(body):
        def step(i, carry):
            body(i, pl.ds(pl.multiple_of(i * positions, positions), positions))
            return carry

        lax.fori_loop(0, slots, step, 0, unroll=UNROLL)

    def score(i, at):
        for p in range(pairs):
            _, _, q_at, k_at = blocks(p)
            scores_ref[at, blocks(p)[0]] = dot(
                proj_ref[at, q_at], spread(proj_ref[at, k_at]), ((1,), (1,))
            )

    def weigh(i, at):
        length = length_ref[i]
        inverse = 1.0 / jnp.maximum(length, 1).astype(F32)
        source = lax.broadcasted_iota(jnp.int32, (positions, features), 1) % half
        time = lax.broadcasted_iota(jnp.int32, (positions, features), 0)
        allowed = (source <= time) & (source < length)
        scores = scores_ref[at, :] * 0.125
        gate = sigmoid(scores)
        value = scores * gate
        weights_ref[at, :] = jnp.where(allowed, value * inverse, 0.0).astype(BF16)
        slopes = (gate + value * (1.0 - gate)) * (inverse * 0.125)
        scores_ref[at, :] = jnp.where(allowed, slopes, 0.0)

    def mix(i, at):
        for p in range(pairs):
            here, v_at, _, _ = blocks(p)
            mixed_ref[at, here] = dot(weights_ref[at, here], spread(proj_ref[at, v_at]))

    def turn(i, at):
        normed, scale = normalised(mixed_ref[at, :])
        dgated = dgated_ref[at, :].astype(F32)
        dpre_ref[at, :features] = (dgated * normed * slope_ref[at, :features]).astype(BF16)
        dmixed = norm_backward(dgated * proj_ref[at, :features].astype(F32), normed, scale)
        dmixed_ref[at, :] = dmixed.astype(BF16)

    def value_back(i, at):
        for p in range(pairs):
            here, v_at, _, _ = blocks(p)
            down = dmixed_ref[at, here]
            dweights = dot(down, spread(proj_ref[at, v_at]), ((1,), (1,)))
            dscores_ref[at, here] = (dweights * scores_ref[at, here]).astype(BF16)
            dv = dot(weights_ref[at, here], down, ((0,), (0,)))
            dv = jnp.where(first, dv[:half], dv[half:])
            dpre_ref[at, v_at] = (dv * slope_ref[at, v_at]).astype(BF16)

    def score_back(i, at):
        for p in range(pairs):
            here, _, q_at, k_at = blocks(p)
            dq = dot(dscores_ref[at, here], spread(proj_ref[at, k_at]))
            dk = dot(dscores_ref[at, here], proj_ref[at, q_at], ((0,), (0,)))
            dk = jnp.where(first, dk[:half], dk[half:])
            dpre_ref[at, q_at] = (dq * slope_ref[at, q_at]).astype(BF16)
            dpre_ref[at, k_at] = (dk * slope_ref[at, k_at]).astype(BF16)

    for body in (score, weigh, mix, turn, value_back, score_back):
        for_slots(body)

    dpre_copy = pltpu.make_async_copy(dpre_ref, dpre_hbm, sent.at[32])
    dpre_copy.start()
    copies = [dpre_copy, turned_copy]
    other = 1 - lax.axis_index("core")
    for y in range(8):
        half_tiles(other, y, turned_ref, dpre_ref, tiles_ref)
        for x in range(4):
            part = (x, y % 2, slice(None), y // 2)
            copy = pltpu.make_async_copy(
                tiles_ref.at[part], send_hbm.at[part], sent.at[y * 4 + x]
            )
            copy.start()
            copies.append(copy)
    for copy in copies:
        copy.wait()


def half_tiles(core, y, turned_ref, dpre_ref, tiles_ref):
    rows = turned_ref.shape[0] // 2
    mine = pl.ds(pl.multiple_of(core * rows, rows), rows)
    left = lax.broadcasted_iota(jnp.int32, (16, 128), 1) < 64
    block = dot(turned_ref[mine, :], dpre_ref[:, y * 256 : (y + 1) * 256])
    for pair in range(2):
        part = block[:, pair * 128 : (pair + 1) * 128]
        swapped = pltpu.roll(part, 64, 1)
        for z in range(8):
            upper = slice(z * 32, z * 32 + 16)
            lower = slice(z * 32 + 16, z * 32 + 32)
            even = jnp.where(left, part[upper], swapped[lower])
            odd = jnp.where(left, swapped[upper], part[lower])
            for x, tile in ((2 * pair, even), (2 * pair + 1, odd)):
                tiles_ref[x, y % 2, z % 2, y // 2, z // 2] = tile.astype(BF16)


def keep_kernel(turned_ref, dpre_ref, tiles_ref):
    for y in range(8):
        half_tiles(lax.axis_index("core"), y, turned_ref, dpre_ref, tiles_ref)


def history_kernel(
    length_ref,
    hist_hbm,
    cot_hbm,
    win_hbm,
    dpre_hbm,
    after_ref,
    out_ref,
    hist_ref,
    cot_ref,
    win_ref,
    dpre_ref,
    grad_ref,
    arrived,
):
    slots, positions, features = hist_ref.shape
    copies = []

    def fetch(source, target):
        copies.append(pltpu.make_async_copy(source, target, arrived.at[len(copies)]))
        copies[-1].start()

    parts = [slice(j * features, (j + 1) * features) for j in range(4)]
    for part in parts:
        fetch(dpre_hbm.at[:, part], dpre_ref.at[:, part])
        fetch(win_hbm.at[:, part], win_ref.at[:, part])
    fetch(hist_hbm, hist_ref)
    fetch(cot_hbm, cot_ref)
    for j, part in enumerate(parts):
        copies[2 * j].wait()
        copies[2 * j + 1].wait()
        share = dot(dpre_ref[:, part], win_ref[:, part], ((1,), (1,)))
        grad_ref[...] = share if j == 0 else grad_ref[...] + share
    copies[-2].wait()
    copies[-1].wait()

    def finish(i, carry):
        at = pl.ds(pl.multiple_of(i * positions, positions), positions)
        normed, scale = normalised(hist_ref[i].astype(F32))
        row = lax.broadcasted_iota(jnp.int32, (positions, features), 0)
        seed = jnp.where(row < length_ref[i], cot_ref[i].astype(F32), 0.0)
        out_ref[i] = (seed + norm_backward(grad_ref[at, :], normed, scale)).astype(BF16)
        return carry

    lax.fori_loop(0, slots, finish, 0, unroll=UNROLL)


def pair_kernel(one_ref, other_ref, out_ref):
    step = 16

    def add(i, carry):
        at = pl.ds(i * step, step)
        out_ref[at] = (one_ref[at].astype(F32) + other_ref[at].astype(F32)).astype(BF16)
        return carry

    lax.fori_loop(0, out_ref.shape[0] // step, add, 0)


def sum_kernel(parts_ref, out_ref, done_ref):
    parts, count = parts_ref.shape[:2]
    step = 4

    def add(i, carry):
        at = pl.ds(i * step, step)
        total = parts_ref[0, at].astype(F32)
        for p in range(1, parts):
            total += parts_ref[p, at].astype(F32)
        out_ref[at] = total.astype(BF16)
        return carry

    lax.fori_loop(0, count // step, add, 0)
    done_ref[...] = jnp.zeros_like(done_ref)


def last_kernel(parts_ref, out_ref):
    total = parts_ref[0, 0].astype(F32)
    for p in range(1, parts_ref.shape[0]):
        total += parts_ref[p, 0].astype(F32)
    out_ref[:16, :] = total[:, :64]
    out_ref[16:, :] = total[:, 64:]


VMEM = pl.BlockSpec(memory_space=pltpu.VMEM)
SMEM = pl.BlockSpec(memory_space=pltpu.SMEM)
HBM = pl.BlockSpec(memory_space=pltpu.HBM)
TILES = (4, 2, 2, 4, 4, 16, 128)
ANY = pl.BlockSpec(memory_space=pl.ANY)
DONE = jax.ShapeDtypeStruct((8, 128), F32)


def weight_tiles(lengths, hist, cot, w_in, w_out):
    slots, positions, features = hist.shape
    rows = slots * positions
    return pl.pallas_call(
        weight_kernel,
        out_shape=(
            jax.ShapeDtypeStruct(TILES, BF16),
            jax.ShapeDtypeStruct((features, rows), BF16),
            jax.ShapeDtypeStruct((rows, 4 * features), BF16),
        ),
        in_specs=[SMEM, HBM, HBM, HBM, HBM],
        out_specs=(HBM, HBM, HBM),
        scratch_shapes=[
            pltpu.VMEM(TILES, BF16),
            pltpu.VMEM((rows, 4 * features), BF16),
            pltpu.VMEM(hist.shape, BF16),
            pltpu.VMEM(hist.shape, BF16),
            pltpu.VMEM(w_in.shape, BF16),
            pltpu.VMEM(w_out.shape, BF16),
            pltpu.VMEM((rows, features), BF16),
            pltpu.VMEM((features, rows), BF16),
            pltpu.VMEM((rows, features), BF16),
            pltpu.VMEM((rows, 4 * features), BF16),
            pltpu.VMEM((rows, 4 * features), F32),
            pltpu.VMEM((rows, features), F32),
            pltpu.VMEM((rows, features), BF16),
            pltpu.VMEM((rows, features), F32),
            pltpu.VMEM((rows, features), BF16),
            pltpu.VMEM((rows, features), BF16),
            pltpu.VMEM((rows, features), BF16),
            pltpu.SemaphoreType.DMA((7,)),
            pltpu.SemaphoreType.DMA((34,)),
        ],
        compiler_params=pltpu.CompilerParams(vmem_limit_bytes=56 * 2**20),
        cost_estimate=pl.CostEstimate(
            flops=2 * rows * features * features * 9, bytes_accessed=8 * 2**20, transcendentals=10**6
        ),
    )(lengths, hist, cot, w_in, w_out)


def kept_tiles(turned, dpre):
    return pl.pallas_call(
        keep_kernel,
        out_shape=jax.ShapeDtypeStruct(TILES, BF16),
        in_specs=[VMEM, VMEM],
        out_specs=VMEM,
        compiler_params=pltpu.CompilerParams(vmem_limit_bytes=12 * 2**20),
        cost_estimate=pl.CostEstimate(
            flops=turned.shape[0] * dpre.shape[0] * dpre.shape[1],
            bytes_accessed=3 * 2**20,
            transcendentals=0,
        ),
    )(turned, dpre)


def history_grads(lengths, hist, cot, w_in, dpre, after):
    rows = dpre.shape[0]
    return pl.pallas_call(
        history_kernel,
        out_shape=jax.ShapeDtypeStruct(hist.shape, BF16),
        in_specs=[SMEM, HBM, HBM, HBM, HBM, ANY],
        out_specs=VMEM,
        scratch_shapes=[
            pltpu.VMEM(hist.shape, BF16),
            pltpu.VMEM(hist.shape, BF16),
            pltpu.VMEM(w_in.shape, BF16),
            pltpu.VMEM(dpre.shape, BF16),
            pltpu.VMEM((rows, hist.shape[-1]), F32),
            pltpu.SemaphoreType.DMA((10,)),
        ],
        compiler_params=pltpu.CompilerParams(vmem_limit_bytes=56 * 2**20),
        cost_estimate=pl.CostEstimate(
            flops=2 * rows * dpre.shape[1] * hist.shape[-1],
            bytes_accessed=6 * 2**20,
            transcendentals=1000,
        ),
    )(lengths, hist, cot, w_in, dpre, after)


def pair_sum(one, other):
    return pl.pallas_call(
        pair_kernel,
        out_shape=jax.ShapeDtypeStruct(one.shape, BF16),
        in_specs=[VMEM, VMEM],
        out_specs=VMEM,
        compiler_params=pltpu.CompilerParams(vmem_limit_bytes=8 * 2**20),
    )(one, other)


def summed(parts):
    return pl.pallas_call(
        sum_kernel,
        out_shape=(jax.ShapeDtypeStruct(parts.shape[1:], BF16), DONE),
        in_specs=[VMEM],
        out_specs=(VMEM, VMEM),
        compiler_params=pltpu.CompilerParams(vmem_limit_bytes=8 * 2**20),
    )(parts)


def last_sum(parts):
    return pl.pallas_call(
        last_kernel,
        out_shape=jax.ShapeDtypeStruct((32, 64), F32),
        in_specs=[VMEM],
        out_specs=VMEM,
        compiler_params=pltpu.CompilerParams(vmem_limit_bytes=2 * 2**20),
    )(parts)


def exchanged(tiles, axes):
    return lax.all_to_all(tiles, axes, 0, 0, tiled=True)


def shards(histories, cotangents, lengths, w_in, w_out):
    hist, cot, slot_lengths = histories[0, 0], cotangents[0, 0], lengths[0, 0]
    send, turned, dpre = weight_tiles(slot_lengths, hist, cot, w_in, w_out)
    other = lax.ppermute(send.reshape(256, 16, 128), "core", [(0, 1), (1, 0)])
    keep = kept_tiles(turned, dpre)
    tiles = pair_sum(keep.reshape(256, 16, 128), other)
    tiles, done = summed(exchanged(tiles.reshape(16, 16, 16, 128), ("x", "yl", "zl")))
    grads = history_grads(slot_lengths, hist, cot, w_in, dpre, done)
    block = last_sum(exchanged(tiles.reshape(16, 1, 16, 128), ("yh", "zh")))
    return (grads[None, None], block)


def solution(mesh):
    torus = Mesh(mesh.devices.reshape(4, 2, 4, 4, 2, 2), AXES)
    seq, rep = ("yh", "yl", "x"), ("zh", "zl", "core")
    placed = (
        P(rep, seq, None, None, None),
        P(rep, seq, None, None, None),
        P(rep, seq, None),
        P(),
        P(),
    )
    return jax.shard_map(
        shards,
        mesh=torus,
        in_specs=placed,
        out_specs=(P(rep, seq, None, None, None), P(rep, seq)),
        check_vma=False,
    )
```

```python
import jax
import jax.numpy as jnp
from jax import lax
from jax.experimental import pallas as pl
from jax.experimental.pallas import tpu as pltpu
from jax.sharding import Mesh
from jax.sharding import PartitionSpec as P

HEADS = 8
EPS = 1e-06
UNROLL = 6
AXES = ("yh", "yl", "x", "zh", "zl", "core")
F32 = jnp.float32
BF16 = jnp.bfloat16


def dot(a, b, contract=((1,), (0,))):
    return lax.dot_general(a, b, (contract, ((), ())), preferred_element_type=F32)


def sigmoid(values):
    return 0.5 * jnp.tanh(0.5 * values) + 0.5


def normalised(values):
    average = jnp.mean(values, axis=-1, keepdims=True)
    centered = values - average
    spread = jnp.mean(centered * centered, axis=-1, keepdims=True)
    scale = lax.rsqrt(spread + EPS)
    return centered * scale, scale


def norm_backward(grad, normed, scale):
    first = jnp.mean(grad, axis=-1, keepdims=True)
    second = jnp.mean(grad * normed, axis=-1, keepdims=True)
    return scale * (grad - first - normed * second)


def weight_kernel(
    length_ref,
    hist_hbm,
    cot_hbm,
    win_hbm,
    wout_hbm,
    send_hbm,
    turned_hbm,
    dpre_hbm,
    tiles_ref,
    dpre_ref,
    hist_ref,
    cot_ref,
    win_ref,
    wout_ref,
    normed_ref,
    turned_ref,
    seed_ref,
    proj_ref,
    slope_ref,
    mixed_ref,
    dgated_ref,
    scores_ref,
    weights_ref,
    dmixed_ref,
    dscores_ref,
    arrived,
    sent,
):
    slots, positions, features = hist_ref.shape
    pairs = features // 128
    half = positions

    started = []

    def fetch(source, target):
        copy = pltpu.make_async_copy(source, target, arrived.at[len(started)])
        copy.start()
        started.append(copy)
        return copy

    hist_copy = fetch(hist_hbm, hist_ref)
    width = 256
    quarters = [slice(j * features // 4, (j + 1) * features // 4) for j in range(4)]
    win_copies = [fetch(win_hbm.at[part, :], win_ref.at[part, :]) for part in quarters]
    cot_copy = fetch(cot_hbm, cot_ref)
    wout_copy = fetch(wout_hbm, wout_ref)

    hist_copy.wait()
    for i in range(slots):
        normed, _ = normalised(hist_ref[i].astype(F32))
        normed_ref[i * positions : (i + 1) * positions, :] = normed.astype(BF16)
    turned = normed_ref[...].T
    for r in range(16):
        place = (r % 2) * 8 + r // 2
        turned_ref[place * 32 : (place + 1) * 32, :] = turned[r * 32 : (r + 1) * 32, :]
    turned_copy = pltpu.make_async_copy(turned_ref, turned_hbm, sent.at[32])
    turned_copy.start()

    for copy in win_copies:
        copy.wait()
    for j in range(4 * features // width):
        columns = slice(j * width, (j + 1) * width)
        pre = dot(normed_ref[...], win_ref[:, columns])
        gate = sigmoid(pre)
        value = pre * gate
        proj_ref[:, columns] = value.astype(BF16)
        slope_ref[:, columns] = gate + value * (1.0 - gate)
    cot_copy.wait()
    row = lax.broadcasted_iota(jnp.int32, (positions, features), 0)
    for i in range(slots):
        seed = jnp.where(row < length_ref[i], cot_ref[i].astype(F32), 0.0)
        seed_ref[i * positions : (i + 1) * positions, :] = seed.astype(BF16)
    wout_copy.wait()
    dgated_ref[...] = dot(seed_ref[...], wout_ref[...], ((1,), (1,))).astype(BF16)

    lane = lax.broadcasted_iota(jnp.int32, (positions, 128), 1)
    first = lane < half
    early = jnp.where(first, 1.0, 0.0).astype(BF16)
    late = jnp.where(first, 0.0, 1.0).astype(BF16)

    def spread(block):
        return jnp.concatenate([block * early, block * late], 0)

    def blocks(p):
        return [slice(b * features + p * 128, b * features + (p + 1) * 128) for b in range(4)]

    def for_slots(body):
        def step(i, carry):
            body(i, pl.ds(pl.multiple_of(i * positions, positions), positions))
            return carry

        lax.fori_loop(0, slots, step, 0, unroll=UNROLL)

    def score(i, at):
        for p in range(pairs):
            _, _, q_at, k_at = blocks(p)
            scores_ref[at, blocks(p)[0]] = dot(
                proj_ref[at, q_at], spread(proj_ref[at, k_at]), ((1,), (1,))
            )

    def weigh(i, at):
        length = length_ref[i]
        inverse = 1.0 / jnp.maximum(length, 1).astype(F32)
        source = lax.broadcasted_iota(jnp.int32, (positions, features), 1) % half
        time = lax.broadcasted_iota(jnp.int32, (positions, features), 0)
        allowed = (source <= time) & (source < length)
        scores = scores_ref[at, :] * 0.125
        gate = sigmoid(scores)
        value = scores * gate
        weights_ref[at, :] = jnp.where(allowed, value * inverse, 0.0).astype(BF16)
        slopes = (gate + value * (1.0 - gate)) * (inverse * 0.125)
        scores_ref[at, :] = jnp.where(allowed, slopes, 0.0)

    def mix(i, at):
        for p in range(pairs):
            here, v_at, _, _ = blocks(p)
            mixed_ref[at, here] = dot(weights_ref[at, here], spread(proj_ref[at, v_at]))

    def turn(i, at):
        normed, scale = normalised(mixed_ref[at, :])
        dgated = dgated_ref[at, :].astype(F32)
        dpre_ref[at, :features] = (dgated * normed * slope_ref[at, :features]).astype(BF16)
        dmixed = norm_backward(dgated * proj_ref[at, :features].astype(F32), normed, scale)
        dmixed_ref[at, :] = dmixed.astype(BF16)

    def value_back(i, at):
        for p in range(pairs):
            here, v_at, _, _ = blocks(p)
            down = dmixed_ref[at, here]
            dweights = dot(down, spread(proj_ref[at, v_at]), ((1,), (1,)))
            dscores_ref[at, here] = (dweights * scores_ref[at, here]).astype(BF16)
            dv = dot(weights_ref[at, here], down, ((0,), (0,)))
            dv = jnp.where(first, dv[:half], dv[half:])
            dpre_ref[at, v_at] = (dv * slope_ref[at, v_at]).astype(BF16)

    def score_back(i, at):
        for p in range(pairs):
            here, _, q_at, k_at = blocks(p)
            dq = dot(dscores_ref[at, here], spread(proj_ref[at, k_at]))
            dk = dot(dscores_ref[at, here], proj_ref[at, q_at], ((0,), (0,)))
            dk = jnp.where(first, dk[:half], dk[half:])
            dpre_ref[at, q_at] = (dq * slope_ref[at, q_at]).astype(BF16)
            dpre_ref[at, k_at] = (dk * slope_ref[at, k_at]).astype(BF16)

    copies = [turned_copy]

    def send_on(first_column, end_column):
        part = (slice(None), slice(first_column, end_column))
        copy = pltpu.make_async_copy(
            dpre_ref.at[part], dpre_hbm.at[part], sent.at[32 + len(copies)]
        )
        copy.start()
        copies.append(copy)

    for body in (score, weigh, mix, turn):
        for_slots(body)
    send_on(0, features)
    for_slots(value_back)
    send_on(features, 2 * features)
    for_slots(score_back)
    send_on(2 * features, 4 * features)

    other = 1 - lax.axis_index("core")
    for y in range(8):
        half_tiles(other, y, turned_ref, dpre_ref, tiles_ref)
        for x in range(4):
            part = (x, y % 2, slice(None), y // 2)
            copy = pltpu.make_async_copy(
                tiles_ref.at[part], send_hbm.at[part], sent.at[y * 4 + x]
            )
            copy.start()
            copies.append(copy)
    for copy in copies:
        copy.wait()


def half_tiles(core, y, turned_ref, dpre_ref, tiles_ref):
    rows = turned_ref.shape[0] // 2
    mine = pl.ds(pl.multiple_of(core * rows, rows), rows)
    left = lax.broadcasted_iota(jnp.int32, (16, 128), 1) < 64
    block = dot(turned_ref[mine, :], dpre_ref[:, y * 256 : (y + 1) * 256])
    for pair in range(2):
        part = block[:, pair * 128 : (pair + 1) * 128]
        swapped = pltpu.roll(part, 64, 1)
        for z in range(8):
            upper = slice(z * 32, z * 32 + 16)
            lower = slice(z * 32 + 16, z * 32 + 32)
            even = jnp.where(left, part[upper], swapped[lower])
            odd = jnp.where(left, swapped[upper], part[lower])
            for x, tile in ((2 * pair, even), (2 * pair + 1, odd)):
                tiles_ref[x, y % 2, z % 2, y // 2, z // 2] = tile.astype(BF16)


def keep_kernel(turned_ref, dpre_ref, tiles_ref):
    for y in range(8):
        half_tiles(lax.axis_index("core"), y, turned_ref, dpre_ref, tiles_ref)


def history_kernel(
    length_ref,
    hist_hbm,
    cot_hbm,
    win_hbm,
    dpre_hbm,
    after_ref,
    out_ref,
    hist_ref,
    cot_ref,
    win_ref,
    dpre_ref,
    grad_ref,
    arrived,
):
    slots, positions, features = hist_ref.shape
    copies = []

    def fetch(source, target):
        copies.append(pltpu.make_async_copy(source, target, arrived.at[len(copies)]))
        copies[-1].start()

    parts = [slice(j * features, (j + 1) * features) for j in range(4)]
    for part in parts:
        fetch(dpre_hbm.at[:, part], dpre_ref.at[:, part])
        fetch(win_hbm.at[:, part], win_ref.at[:, part])
    fetch(hist_hbm, hist_ref)
    fetch(cot_hbm, cot_ref)
    for j, part in enumerate(parts):
        copies[2 * j].wait()
        copies[2 * j + 1].wait()
        share = dot(dpre_ref[:, part], win_ref[:, part], ((1,), (1,)))
        grad_ref[...] = share if j == 0 else grad_ref[...] + share
    copies[-2].wait()
    copies[-1].wait()

    def finish(i, carry):
        at = pl.ds(pl.multiple_of(i * positions, positions), positions)
        normed, scale = normalised(hist_ref[i].astype(F32))
        row = lax.broadcasted_iota(jnp.int32, (positions, features), 0)
        seed = jnp.where(row < length_ref[i], cot_ref[i].astype(F32), 0.0)
        out_ref[i] = (seed + norm_backward(grad_ref[at, :], normed, scale)).astype(BF16)
        return carry

    lax.fori_loop(0, slots, finish, 0, unroll=UNROLL)


def pair_kernel(one_ref, other_ref, out_ref):
    step = 16

    def add(i, carry):
        at = pl.ds(i * step, step)
        out_ref[at] = (one_ref[at].astype(F32) + other_ref[at].astype(F32)).astype(BF16)
        return carry

    lax.fori_loop(0, out_ref.shape[0] // step, add, 0)


def sum_kernel(parts_ref, out_ref):
    parts, count = parts_ref.shape[:2]
    for i in range(count):
        total = parts_ref[0, i].astype(F32)
        for p in range(1, parts):
            total += parts_ref[p, i].astype(F32)
        out_ref[i] = total.astype(BF16)


def last_kernel(parts_ref, out_ref):
    total = parts_ref[0, 0].astype(F32)
    for p in range(1, parts_ref.shape[0]):
        total += parts_ref[p, 0].astype(F32)
    out_ref[:16, :] = total[:, :64]
    out_ref[16:, :] = total[:, 64:]


VMEM = pl.BlockSpec(memory_space=pltpu.VMEM)
SMEM = pl.BlockSpec(memory_space=pltpu.SMEM)
HBM = pl.BlockSpec(memory_space=pltpu.HBM)
TILES = (4, 2, 2, 4, 4, 16, 128)
ANY = pl.BlockSpec(memory_space=pl.ANY)


def weight_tiles(lengths, hist, cot, w_in, w_out):
    slots, positions, features = hist.shape
    rows = slots * positions
    return pl.pallas_call(
        weight_kernel,
        out_shape=(
            jax.ShapeDtypeStruct(TILES, BF16),
            jax.ShapeDtypeStruct((features, rows), BF16),
            jax.ShapeDtypeStruct((rows, 4 * features), BF16),
        ),
        in_specs=[SMEM, HBM, HBM, HBM, HBM],
        out_specs=(HBM, HBM, HBM),
        scratch_shapes=[
            pltpu.VMEM(TILES, BF16),
            pltpu.VMEM((rows, 4 * features), BF16),
            pltpu.VMEM(hist.shape, BF16),
            pltpu.VMEM(hist.shape, BF16),
            pltpu.VMEM(w_in.shape, BF16),
            pltpu.VMEM(w_out.shape, BF16),
            pltpu.VMEM((rows, features), BF16),
            pltpu.VMEM((features, rows), BF16),
            pltpu.VMEM((rows, features), BF16),
            pltpu.VMEM((rows, 4 * features), BF16),
            pltpu.VMEM((rows, 4 * features), F32),
            pltpu.VMEM((rows, features), F32),
            pltpu.VMEM((rows, features), BF16),
            pltpu.VMEM((rows, features), F32),
            pltpu.VMEM((rows, features), BF16),
            pltpu.VMEM((rows, features), BF16),
            pltpu.VMEM((rows, features), BF16),
            pltpu.SemaphoreType.DMA((7,)),
            pltpu.SemaphoreType.DMA((36,)),
        ],
        compiler_params=pltpu.CompilerParams(vmem_limit_bytes=56 * 2**20),
        cost_estimate=pl.CostEstimate(
            flops=2 * rows * features * features * 9, bytes_accessed=8 * 2**20, transcendentals=10**6
        ),
    )(lengths, hist, cot, w_in, w_out)


def kept_tiles(turned, dpre):
    return pl.pallas_call(
        keep_kernel,
        out_shape=jax.ShapeDtypeStruct(TILES, BF16),
        in_specs=[VMEM, VMEM],
        out_specs=VMEM,
        compiler_params=pltpu.CompilerParams(vmem_limit_bytes=12 * 2**20),
        cost_estimate=pl.CostEstimate(
            flops=turned.shape[0] * dpre.shape[0] * dpre.shape[1],
            bytes_accessed=3 * 2**20,
            transcendentals=0,
        ),
    )(turned, dpre)


def history_grads(lengths, hist, cot, w_in, dpre, after):
    rows = dpre.shape[0]
    return pl.pallas_call(
        history_kernel,
        out_shape=jax.ShapeDtypeStruct(hist.shape, BF16),
        in_specs=[SMEM, HBM, HBM, HBM, HBM, ANY],
        out_specs=VMEM,
        scratch_shapes=[
            pltpu.VMEM(hist.shape, BF16),
            pltpu.VMEM(hist.shape, BF16),
            pltpu.VMEM(w_in.shape, BF16),
            pltpu.VMEM(dpre.shape, BF16),
            pltpu.VMEM((rows, hist.shape[-1]), F32),
            pltpu.SemaphoreType.DMA((10,)),
        ],
        compiler_params=pltpu.CompilerParams(vmem_limit_bytes=56 * 2**20),
        cost_estimate=pl.CostEstimate(
            flops=2 * rows * dpre.shape[1] * hist.shape[-1],
            bytes_accessed=6 * 2**20,
            transcendentals=1000,
        ),
    )(lengths, hist, cot, w_in, dpre, after)


def pair_sum(one, other):
    return pl.pallas_call(
        pair_kernel,
        out_shape=jax.ShapeDtypeStruct(one.shape, BF16),
        in_specs=[VMEM, VMEM],
        out_specs=VMEM,
        compiler_params=pltpu.CompilerParams(vmem_limit_bytes=8 * 2**20),
    )(one, other)


def summed(parts):
    return pl.pallas_call(
        sum_kernel,
        out_shape=jax.ShapeDtypeStruct(parts.shape[1:], BF16),
        in_specs=[VMEM],
        out_specs=VMEM,
        compiler_params=pltpu.CompilerParams(vmem_limit_bytes=8 * 2**20),
    )(parts)


def last_sum(parts):
    return pl.pallas_call(
        last_kernel,
        out_shape=jax.ShapeDtypeStruct((32, 64), F32),
        in_specs=[VMEM],
        out_specs=VMEM,
        compiler_params=pltpu.CompilerParams(vmem_limit_bytes=2 * 2**20),
    )(parts)


def exchanged(tiles, axes):
    return lax.all_to_all(tiles, axes, 0, 0, tiled=True)


def shards(histories, cotangents, lengths, w_in, w_out):
    hist, cot, slot_lengths = histories[0, 0], cotangents[0, 0], lengths[0, 0]
    send, turned, dpre = weight_tiles(slot_lengths, hist, cot, w_in, w_out)
    other = lax.ppermute(send.reshape(256, 16, 128), "core", [(0, 1), (1, 0)])
    keep = kept_tiles(turned, dpre)
    tiles = pair_sum(keep.reshape(256, 16, 128), other)
    tiles = summed(exchanged(tiles.reshape(16, 16, 16, 128), ("x", "yl", "zl")))
    grads = history_grads(slot_lengths, hist, cot, w_in, dpre, tiles)
    block = last_sum(exchanged(tiles.reshape(16, 1, 16, 128), ("yh", "zh")))
    return (grads[None, None], block)


def solution(mesh):
    torus = Mesh(mesh.devices.reshape(4, 2, 4, 4, 2, 2), AXES)
    seq, rep = ("yh", "yl", "x"), ("zh", "zl", "core")
    placed = (
        P(rep, seq, None, None, None),
        P(rep, seq, None, None, None),
        P(rep, seq, None),
        P(),
        P(),
    )
    return jax.shard_map(
        shards,
        mesh=torus,
        in_specs=placed,
        out_specs=(P(rep, seq, None, None, None), P(rep, seq)),
        check_vma=False,
    )
```

```python
import jax
import jax.numpy as jnp
from jax import lax
from jax.experimental import pallas as pl
from jax.experimental.pallas import tpu as pltpu
from jax.sharding import Mesh
from jax.sharding import PartitionSpec as P

HEADS = 8
EPS = 1e-06
UNROLL = 6
AXES = ("yh", "yl", "x", "zh", "zl", "core")
F32 = jnp.float32
BF16 = jnp.bfloat16


def dot(a, b, contract=((1,), (0,))):
    return lax.dot_general(a, b, (contract, ((), ())), preferred_element_type=F32)


def sigmoid(values):
    return 0.5 * jnp.tanh(0.5 * values) + 0.5


def normalised(values):
    average = jnp.mean(values, axis=-1, keepdims=True)
    centered = values - average
    spread = jnp.mean(centered * centered, axis=-1, keepdims=True)
    scale = lax.rsqrt(spread + EPS)
    return centered * scale, scale


def norm_backward(grad, normed, scale):
    first = jnp.mean(grad, axis=-1, keepdims=True)
    second = jnp.mean(grad * normed, axis=-1, keepdims=True)
    return scale * (grad - first - normed * second)


def weight_kernel(
    length_ref,
    hist_hbm,
    cot_hbm,
    win_hbm,
    wout_hbm,
    send_hbm,
    both_hbm,
    tiles_ref,
    both_ref,
    hist_ref,
    cot_ref,
    win_ref,
    wout_ref,
    normed_ref,
    seed_ref,
    proj_ref,
    slope_ref,
    mixed_ref,
    dgated_ref,
    scores_ref,
    weights_ref,
    dmixed_ref,
    dscores_ref,
    arrived,
    sent,
):
    slots, positions, features = hist_ref.shape
    pairs = features // 128
    half = positions
    rows = slots * positions
    dpre_ref = both_ref.at[:rows]

    started = []

    def fetch(source, target):
        copy = pltpu.make_async_copy(source, target, arrived.at[len(started)])
        copy.start()
        started.append(copy)
        return copy

    hist_copy = fetch(hist_hbm, hist_ref)
    width = 256
    quarters = [slice(j * features // 4, (j + 1) * features // 4) for j in range(4)]
    win_copies = [fetch(win_hbm.at[part, :], win_ref.at[part, :]) for part in quarters]
    cot_copy = fetch(cot_hbm, cot_ref)
    wout_copy = fetch(wout_hbm, wout_ref)

    hist_copy.wait()
    for i in range(slots):
        normed, _ = normalised(hist_ref[i].astype(F32))
        normed_ref[i * positions : (i + 1) * positions, :] = normed.astype(BF16)
    turned = normed_ref[...].T
    for r in range(16):
        place = (r % 2) * 8 + r // 2
        at, column = rows + place % 4 * 32, place // 4 * rows
        both_ref[at : at + 32, column : column + rows] = turned[r * 32 : (r + 1) * 32, :]
    below = (slice(rows, rows + 128), slice(0, 4 * rows))
    turned_copy = pltpu.make_async_copy(both_ref.at[below], both_hbm.at[below], sent.at[32])
    turned_copy.start()

    for copy in win_copies:
        copy.wait()
    for j in range(4 * features // width):
        columns = slice(j * width, (j + 1) * width)
        pre = dot(normed_ref[...], win_ref[:, columns])
        gate = sigmoid(pre)
        value = pre * gate
        proj_ref[:, columns] = value.astype(BF16)
        slope_ref[:, columns] = gate + value * (1.0 - gate)
    cot_copy.wait()
    row = lax.broadcasted_iota(jnp.int32, (positions, features), 0)
    for i in range(slots):
        seed = jnp.where(row < length_ref[i], cot_ref[i].astype(F32), 0.0)
        seed_ref[i * positions : (i + 1) * positions, :] = seed.astype(BF16)
    wout_copy.wait()
    dgated_ref[...] = dot(seed_ref[...], wout_ref[...], ((1,), (1,))).astype(BF16)

    lane = lax.broadcasted_iota(jnp.int32, (positions, 128), 1)
    first = lane < half
    early = jnp.where(first, 1.0, 0.0).astype(BF16)
    late = jnp.where(first, 0.0, 1.0).astype(BF16)

    def spread(block):
        return jnp.concatenate([block * early, block * late], 0)

    def blocks(p):
        return [slice(b * features + p * 128, b * features + (p + 1) * 128) for b in range(4)]

    def for_slots(body):
        def step(i, carry):
            body(i, pl.ds(pl.multiple_of(i * positions, positions), positions))
            return carry

        lax.fori_loop(0, slots, step, 0, unroll=UNROLL)

    def score(i, at):
        for p in range(pairs):
            _, _, q_at, k_at = blocks(p)
            scores_ref[at, blocks(p)[0]] = dot(
                proj_ref[at, q_at], spread(proj_ref[at, k_at]), ((1,), (1,))
            )

    def weigh(i, at):
        length = length_ref[i]
        inverse = 1.0 / jnp.maximum(length, 1).astype(F32)
        source = lax.broadcasted_iota(jnp.int32, (positions, features), 1) % half
        time = lax.broadcasted_iota(jnp.int32, (positions, features), 0)
        allowed = (source <= time) & (source < length)
        scores = scores_ref[at, :] * 0.125
        gate = sigmoid(scores)
        value = scores * gate
        weights_ref[at, :] = jnp.where(allowed, value * inverse, 0.0).astype(BF16)
        slopes = (gate + value * (1.0 - gate)) * (inverse * 0.125)
        scores_ref[at, :] = jnp.where(allowed, slopes, 0.0)

    def mix(i, at):
        for p in range(pairs):
            here, v_at, _, _ = blocks(p)
            mixed_ref[at, here] = dot(weights_ref[at, here], spread(proj_ref[at, v_at]))

    def turn(i, at):
        normed, scale = normalised(mixed_ref[at, :])
        dgated = dgated_ref[at, :].astype(F32)
        dpre_ref[at, :features] = (dgated * normed * slope_ref[at, :features]).astype(BF16)
        dmixed = norm_backward(dgated * proj_ref[at, :features].astype(F32), normed, scale)
        dmixed_ref[at, :] = dmixed.astype(BF16)

    def value_back(i, at):
        for p in range(pairs):
            here, v_at, _, _ = blocks(p)
            down = dmixed_ref[at, here]
            dweights = dot(down, spread(proj_ref[at, v_at]), ((1,), (1,)))
            dscores_ref[at, here] = (dweights * scores_ref[at, here]).astype(BF16)
            dv = dot(weights_ref[at, here], down, ((0,), (0,)))
            dv = jnp.where(first, dv[:half], dv[half:])
            dpre_ref[at, v_at] = (dv * slope_ref[at, v_at]).astype(BF16)

    def score_back(i, at):
        for p in range(pairs):
            here, _, q_at, k_at = blocks(p)
            dq = dot(dscores_ref[at, here], spread(proj_ref[at, k_at]))
            dk = dot(dscores_ref[at, here], proj_ref[at, q_at], ((0,), (0,)))
            dk = jnp.where(first, dk[:half], dk[half:])
            dpre_ref[at, q_at] = (dq * slope_ref[at, q_at]).astype(BF16)
            dpre_ref[at, k_at] = (dk * slope_ref[at, k_at]).astype(BF16)

    copies = [turned_copy]

    def send_on(first_column, end_column):
        part = (slice(0, rows), slice(first_column, end_column))
        copy = pltpu.make_async_copy(
            both_ref.at[part], both_hbm.at[part], sent.at[32 + len(copies)]
        )
        copy.start()
        copies.append(copy)

    for body in (score, weigh, mix, turn):
        for_slots(body)
    send_on(0, features)
    for_slots(value_back)
    send_on(features, 2 * features)
    for_slots(score_back)
    send_on(2 * features, 4 * features)

    other = 1 - lax.axis_index("core")
    for y in range(8):
        half_tiles(other, y, both_ref, tiles_ref)
        for x in range(4):
            part = (x, y % 2, slice(None), y // 2)
            copy = pltpu.make_async_copy(
                tiles_ref.at[part], send_hbm.at[part], sent.at[y * 4 + x]
            )
            copy.start()
            copies.append(copy)
    for copy in copies:
        copy.wait()


def half_tiles(core, y, both_ref, tiles_ref):
    rows = both_ref.shape[0] - 128
    left = lax.broadcasted_iota(jnp.int32, (16, 128), 1) < 64
    turned = jnp.concatenate(
        [
            both_ref[rows:, pl.ds(pl.multiple_of((2 * core + k) * rows, rows), rows)]
            for k in range(2)
        ],
        0,
    )
    block = dot(turned, both_ref[:rows, y * 256 : (y + 1) * 256])
    for pair in range(2):
        part = block[:, pair * 128 : (pair + 1) * 128]
        swapped = pltpu.roll(part, 64, 1)
        for z in range(8):
            upper = slice(z * 32, z * 32 + 16)
            lower = slice(z * 32 + 16, z * 32 + 32)
            even = jnp.where(left, part[upper], swapped[lower])
            odd = jnp.where(left, swapped[upper], part[lower])
            for x, tile in ((2 * pair, even), (2 * pair + 1, odd)):
                tiles_ref[x, y % 2, z % 2, y // 2, z // 2] = tile.astype(BF16)


def keep_kernel(both_ref, tiles_ref):
    for y in range(8):
        half_tiles(lax.axis_index("core"), y, both_ref, tiles_ref)


def history_kernel(
    length_ref,
    hist_hbm,
    cot_hbm,
    win_hbm,
    both_hbm,
    after_ref,
    out_ref,
    hist_ref,
    cot_ref,
    win_ref,
    dpre_ref,
    grad_ref,
    arrived,
):
    slots, positions, features = hist_ref.shape
    copies = []

    def fetch(source, target):
        copies.append(pltpu.make_async_copy(source, target, arrived.at[len(copies)]))
        copies[-1].start()

    parts = [slice(j * features, (j + 1) * features) for j in range(4)]
    for part in parts:
        fetch(both_hbm.at[: slots * positions, part], dpre_ref.at[:, part])
        fetch(win_hbm.at[:, part], win_ref.at[:, part])
    fetch(hist_hbm, hist_ref)
    fetch(cot_hbm, cot_ref)
    for j, part in enumerate(parts):
        copies[2 * j].wait()
        copies[2 * j + 1].wait()
        share = dot(dpre_ref[:, part], win_ref[:, part], ((1,), (1,)))
        grad_ref[...] = share if j == 0 else grad_ref[...] + share
    copies[-2].wait()
    copies[-1].wait()

    def finish(i, carry):
        at = pl.ds(pl.multiple_of(i * positions, positions), positions)
        normed, scale = normalised(hist_ref[i].astype(F32))
        row = lax.broadcasted_iota(jnp.int32, (positions, features), 0)
        seed = jnp.where(row < length_ref[i], cot_ref[i].astype(F32), 0.0)
        out_ref[i] = (seed + norm_backward(grad_ref[at, :], normed, scale)).astype(BF16)
        return carry

    lax.fori_loop(0, slots, finish, 0, unroll=UNROLL)


def pair_kernel(one_ref, other_ref, out_ref):
    step = 16

    def add(i, carry):
        at = pl.ds(i * step, step)
        out_ref[at] = (one_ref[at].astype(F32) + other_ref[at].astype(F32)).astype(BF16)
        return carry

    lax.fori_loop(0, out_ref.shape[0] // step, add, 0)


def sum_kernel(parts_ref, out_ref):
    parts, count = parts_ref.shape[:2]
    for i in range(count):
        total = parts_ref[0, i].astype(F32)
        for p in range(1, parts):
            total += parts_ref[p, i].astype(F32)
        out_ref[i] = total.astype(BF16)


def last_kernel(parts_ref, out_ref):
    total = parts_ref[0, 0].astype(F32)
    for p in range(1, parts_ref.shape[0]):
        total += parts_ref[p, 0].astype(F32)
    out_ref[:16, :] = total[:, :64]
    out_ref[16:, :] = total[:, 64:]


VMEM = pl.BlockSpec(memory_space=pltpu.VMEM)
SMEM = pl.BlockSpec(memory_space=pltpu.SMEM)
HBM = pl.BlockSpec(memory_space=pltpu.HBM)
TILES = (4, 2, 2, 4, 4, 16, 128)
ANY = pl.BlockSpec(memory_space=pl.ANY)


def weight_tiles(lengths, hist, cot, w_in, w_out):
    slots, positions, features = hist.shape
    rows = slots * positions
    return pl.pallas_call(
        weight_kernel,
        out_shape=(
            jax.ShapeDtypeStruct(TILES, BF16),
            jax.ShapeDtypeStruct((rows + 128, 4 * features), BF16),
        ),
        in_specs=[SMEM, HBM, HBM, HBM, HBM],
        out_specs=(HBM, HBM),
        scratch_shapes=[
            pltpu.VMEM(TILES, BF16),
            pltpu.VMEM((rows + 128, 4 * features), BF16),
            pltpu.VMEM(hist.shape, BF16),
            pltpu.VMEM(hist.shape, BF16),
            pltpu.VMEM(w_in.shape, BF16),
            pltpu.VMEM(w_out.shape, BF16),
            pltpu.VMEM((rows, features), BF16),
            pltpu.VMEM((rows, features), BF16),
            pltpu.VMEM((rows, 4 * features), BF16),
            pltpu.VMEM((rows, 4 * features), F32),
            pltpu.VMEM((rows, features), F32),
            pltpu.VMEM((rows, features), BF16),
            pltpu.VMEM((rows, features), F32),
            pltpu.VMEM((rows, features), BF16),
            pltpu.VMEM((rows, features), BF16),
            pltpu.VMEM((rows, features), BF16),
            pltpu.SemaphoreType.DMA((7,)),
            pltpu.SemaphoreType.DMA((36,)),
        ],
        compiler_params=pltpu.CompilerParams(vmem_limit_bytes=56 * 2**20),
        cost_estimate=pl.CostEstimate(
            flops=2 * rows * features * features * 9, bytes_accessed=8 * 2**20, transcendentals=10**6
        ),
    )(lengths, hist, cot, w_in, w_out)


def kept_tiles(both):
    return pl.pallas_call(
        keep_kernel,
        out_shape=jax.ShapeDtypeStruct(TILES, BF16),
        in_specs=[VMEM],
        out_specs=VMEM,
        compiler_params=pltpu.CompilerParams(vmem_limit_bytes=12 * 2**20),
        cost_estimate=pl.CostEstimate(
            flops=both.shape[0] * both.shape[1] * 512,
            bytes_accessed=3 * 2**20,
            transcendentals=0,
        ),
    )(both)


def history_grads(lengths, hist, cot, w_in, both, after):
    rows = hist.shape[0] * hist.shape[1]
    return pl.pallas_call(
        history_kernel,
        out_shape=jax.ShapeDtypeStruct(hist.shape, BF16),
        in_specs=[SMEM, HBM, HBM, HBM, HBM, ANY],
        out_specs=VMEM,
        scratch_shapes=[
            pltpu.VMEM(hist.shape, BF16),
            pltpu.VMEM(hist.shape, BF16),
            pltpu.VMEM(w_in.shape, BF16),
            pltpu.VMEM((rows, w_in.shape[1]), BF16),
            pltpu.VMEM((rows, hist.shape[-1]), F32),
            pltpu.SemaphoreType.DMA((10,)),
        ],
        compiler_params=pltpu.CompilerParams(vmem_limit_bytes=56 * 2**20),
        cost_estimate=pl.CostEstimate(
            flops=2 * rows * w_in.shape[1] * hist.shape[-1],
            bytes_accessed=6 * 2**20,
            transcendentals=1000,
        ),
    )(lengths, hist, cot, w_in, both, after)


def pair_sum(one, other):
    return pl.pallas_call(
        pair_kernel,
        out_shape=jax.ShapeDtypeStruct(one.shape, BF16),
        in_specs=[VMEM, VMEM],
        out_specs=VMEM,
        compiler_params=pltpu.CompilerParams(vmem_limit_bytes=8 * 2**20),
    )(one, other)


def summed(parts):
    return pl.pallas_call(
        sum_kernel,
        out_shape=jax.ShapeDtypeStruct(parts.shape[1:], BF16),
        in_specs=[VMEM],
        out_specs=VMEM,
        compiler_params=pltpu.CompilerParams(vmem_limit_bytes=8 * 2**20),
    )(parts)


def last_sum(parts):
    return pl.pallas_call(
        last_kernel,
        out_shape=jax.ShapeDtypeStruct((32, 64), F32),
        in_specs=[VMEM],
        out_specs=VMEM,
        compiler_params=pltpu.CompilerParams(vmem_limit_bytes=2 * 2**20),
    )(parts)


def exchanged(tiles, axes):
    return lax.all_to_all(tiles, axes, 0, 0, tiled=True)


def shards(histories, cotangents, lengths, w_in, w_out):
    hist, cot, slot_lengths = histories[0, 0], cotangents[0, 0], lengths[0, 0]
    send, both = weight_tiles(slot_lengths, hist, cot, w_in, w_out)
    other = lax.ppermute(send.reshape(256, 16, 128), "core", [(0, 1), (1, 0)])
    keep = kept_tiles(both)
    tiles = pair_sum(keep.reshape(256, 16, 128), other)
    tiles = summed(exchanged(tiles.reshape(16, 16, 16, 128), ("x", "yl", "zl")))
    grads = history_grads(slot_lengths, hist, cot, w_in, both, tiles)
    block = last_sum(exchanged(tiles.reshape(16, 1, 16, 128), ("yh", "zh")))
    return (grads[None, None], block)


def solution(mesh):
    torus = Mesh(mesh.devices.reshape(4, 2, 4, 4, 2, 2), AXES)
    seq, rep = ("yh", "yl", "x"), ("zh", "zl", "core")
    placed = (
        P(rep, seq, None, None, None),
        P(rep, seq, None, None, None),
        P(rep, seq, None),
        P(),
        P(),
    )
    return jax.shard_map(
        shards,
        mesh=torus,
        in_specs=placed,
        out_specs=(P(rep, seq, None, None, None), P(rep, seq)),
        check_vma=False,
    )
```

```python
import jax
import jax.numpy as jnp
from jax import lax
from jax.experimental import pallas as pl
from jax.experimental.pallas import tpu as pltpu
from jax.sharding import Mesh
from jax.sharding import PartitionSpec as P

HEADS = 8
EPS = 1e-06
LIGHT = 4
AXES = ("yh", "yl", "x", "zh", "zl", "core")
F32 = jnp.float32
BF16 = jnp.bfloat16


def dot(a, b, contract=((1,), (0,))):
    return lax.dot_general(a, b, (contract, ((), ())), preferred_element_type=F32)


def sigmoid(values):
    return 0.5 * jnp.tanh(0.5 * values) + 0.5


def normalised(values):
    average = jnp.mean(values, axis=-1, keepdims=True)
    centered = values - average
    spread = jnp.mean(centered * centered, axis=-1, keepdims=True)
    scale = lax.rsqrt(spread + EPS)
    return centered * scale, scale


def norm_backward(grad, normed, scale):
    first = jnp.mean(grad, axis=-1, keepdims=True)
    second = jnp.mean(grad * normed, axis=-1, keepdims=True)
    return scale * (grad - first - normed * second)


def slot_order(length_ref, slots):
    live = [jnp.where(length_ref[i] > 0, 1, 0) for i in range(slots)]
    count = sum(live)
    ahead, behind, places = 0, count, []
    for i in range(slots):
        places.append(jnp.where(live[i] > 0, ahead, behind))
        ahead, behind = ahead + live[i], behind + 1 - live[i]
    order = [sum(jnp.where(places[i] == n, i, 0) for i in range(slots)) for n in range(slots)]
    return count, places, order


def weight_kernel(
    length_ref,
    hist_hbm,
    cot_hbm,
    win_hbm,
    wout_hbm,
    send_hbm,
    both_hbm,
    tiles_ref,
    both_ref,
    hist_ref,
    cot_ref,
    win_ref,
    wout_ref,
    normed_ref,
    seed_ref,
    proj_ref,
    slope_ref,
    mixed_ref,
    dgated_ref,
    scores_ref,
    weights_ref,
    dmixed_ref,
    dscores_ref,
    sorted_ref,
    arrived,
    sent,
):
    every, positions, features = hist_ref.shape
    pairs = features // 128
    half = positions
    live, _, order = slot_order(length_ref, every)

    def work(slots):
        rows = slots * positions
        dpre_ref = both_ref.at[:rows]
        for i in range(slots):
            sorted_ref[i] = length_ref[order[i] if slots < every else i]
        started = []

        def fetch(source, target):
            copy = pltpu.make_async_copy(source, target, arrived.at[len(started)])
            copy.start()
            started.append(copy)
            return copy

        if slots < every:
            hist_copies = [fetch(hist_hbm.at[order[i]], hist_ref.at[i]) for i in range(slots)]
        else:
            hist_copies = [fetch(hist_hbm, hist_ref)]
        width = 256
        quarters = [slice(j * features // 4, (j + 1) * features // 4) for j in range(4)]
        win_copies = [fetch(win_hbm.at[part, :], win_ref.at[part, :]) for part in quarters]
        if slots < every:
            cot_copies = [fetch(cot_hbm.at[order[i]], cot_ref.at[i]) for i in range(slots)]
        else:
            cot_copies = [fetch(cot_hbm, cot_ref)]
        wout_copy = fetch(wout_hbm, wout_ref)

        for copy in hist_copies:
            copy.wait()
        for i in range(slots):
            normed, _ = normalised(hist_ref[i].astype(F32))
            normed_ref[i * positions : (i + 1) * positions, :] = normed.astype(BF16)
        turned = normed_ref[:rows, :].T
        for r in range(16):
            place = (r % 2) * 8 + r // 2
            at, column = every * positions + place % 4 * 32, place // 4 * every * positions
            both_ref[at : at + 32, column : column + rows] = turned[r * 32 : (r + 1) * 32, :]
        total = every * positions
        below = (slice(total, total + 128), slice(0, 4 * total))
        turned_copy = pltpu.make_async_copy(both_ref.at[below], both_hbm.at[below], sent.at[32])
        turned_copy.start()

        for copy in win_copies:
            copy.wait()
        for j in range(4 * features // width):
            columns = slice(j * width, (j + 1) * width)
            pre = dot(normed_ref[:rows, :], win_ref[:, columns])
            gate = sigmoid(pre)
            value = pre * gate
            proj_ref[:rows, columns] = value.astype(BF16)
            slope_ref[:rows, columns] = gate + value * (1.0 - gate)
        for copy in cot_copies:
            copy.wait()
        row = lax.broadcasted_iota(jnp.int32, (positions, features), 0)
        for i in range(slots):
            seed = jnp.where(row < sorted_ref[i], cot_ref[i].astype(F32), 0.0)
            seed_ref[i * positions : (i + 1) * positions, :] = seed.astype(BF16)
        wout_copy.wait()
        dgated = dot(seed_ref[:rows, :], wout_ref[...], ((1,), (1,)))
        dgated_ref[:rows, :] = dgated.astype(BF16)

        lane = lax.broadcasted_iota(jnp.int32, (positions, 128), 1)
        first = lane < half
        early = jnp.where(first, 1.0, 0.0).astype(BF16)
        late = jnp.where(first, 0.0, 1.0).astype(BF16)

        def spread(block):
            return jnp.concatenate([block * early, block * late], 0)

        def blocks(p):
            return [slice(b * features + p * 128, b * features + (p + 1) * 128) for b in range(4)]

        def for_slots(body):
            def step(i, carry):
                body(i, pl.ds(pl.multiple_of(i * positions, positions), positions))
                return carry

            lax.fori_loop(0, slots, step, 0, unroll=slots)

        def score(i, at):
            for p in range(pairs):
                _, _, q_at, k_at = blocks(p)
                scores_ref[at, blocks(p)[0]] = dot(
                    proj_ref[at, q_at], spread(proj_ref[at, k_at]), ((1,), (1,))
                )

        def weigh(i, at):
            length = sorted_ref[i]
            inverse = 1.0 / jnp.maximum(length, 1).astype(F32)
            source = lax.broadcasted_iota(jnp.int32, (positions, features), 1) % half
            time = lax.broadcasted_iota(jnp.int32, (positions, features), 0)
            allowed = (source <= time) & (source < length)
            scores = scores_ref[at, :] * 0.125
            gate = sigmoid(scores)
            value = scores * gate
            weights_ref[at, :] = jnp.where(allowed, value * inverse, 0.0).astype(BF16)
            slopes = (gate + value * (1.0 - gate)) * (inverse * 0.125)
            scores_ref[at, :] = jnp.where(allowed, slopes, 0.0)

        def mix(i, at):
            for p in range(pairs):
                here, v_at, _, _ = blocks(p)
                mixed_ref[at, here] = dot(weights_ref[at, here], spread(proj_ref[at, v_at]))

        def turn(i, at):
            normed, scale = normalised(mixed_ref[at, :])
            dgated = dgated_ref[at, :].astype(F32)
            dpre_ref[at, :features] = (dgated * normed * slope_ref[at, :features]).astype(BF16)
            dmixed = norm_backward(dgated * proj_ref[at, :features].astype(F32), normed, scale)
            dmixed_ref[at, :] = dmixed.astype(BF16)

        def value_back(i, at):
            for p in range(pairs):
                here, v_at, _, _ = blocks(p)
                down = dmixed_ref[at, here]
                dweights = dot(down, spread(proj_ref[at, v_at]), ((1,), (1,)))
                dscores_ref[at, here] = (dweights * scores_ref[at, here]).astype(BF16)
                dv = dot(weights_ref[at, here], down, ((0,), (0,)))
                dv = jnp.where(first, dv[:half], dv[half:])
                dpre_ref[at, v_at] = (dv * slope_ref[at, v_at]).astype(BF16)

        def score_back(i, at):
            for p in range(pairs):
                here, _, q_at, k_at = blocks(p)
                dq = dot(dscores_ref[at, here], spread(proj_ref[at, k_at]))
                dk = dot(dscores_ref[at, here], proj_ref[at, q_at], ((0,), (0,)))
                dk = jnp.where(first, dk[:half], dk[half:])
                dpre_ref[at, q_at] = (dq * slope_ref[at, q_at]).astype(BF16)
                dpre_ref[at, k_at] = (dk * slope_ref[at, k_at]).astype(BF16)

        copies = [turned_copy]

        def send_on(first_column, end_column):
            part = (slice(0, rows), slice(first_column, end_column))
            copy = pltpu.make_async_copy(
                both_ref.at[part], both_hbm.at[part], sent.at[32 + len(copies)]
            )
            copy.start()
            copies.append(copy)

        for body in (score, weigh, mix, turn):
            for_slots(body)
        send_on(0, features)
        for_slots(value_back)
        send_on(features, 2 * features)
        for_slots(score_back)
        send_on(2 * features, 4 * features)

        other = 1 - lax.axis_index("core")
        for y in range(8):
            half_tiles(other, y, both_ref, tiles_ref, rows)
            for x in range(4):
                part = (x, y % 2, slice(None), y // 2)
                copy = pltpu.make_async_copy(
                    tiles_ref.at[part], send_hbm.at[part], sent.at[y * 4 + x]
                )
                copy.start()
                copies.append(copy)
        for copy in copies:
            copy.wait()

    @pl.when(live <= LIGHT)
    def _():
        work(LIGHT)

    @pl.when(live > LIGHT)
    def _():
        work(every)


def half_tiles(core, y, both_ref, tiles_ref, rows):
    total = both_ref.shape[0] - 128
    left = lax.broadcasted_iota(jnp.int32, (16, 128), 1) < 64
    turned = jnp.concatenate(
        [
            both_ref[total:, pl.ds(pl.multiple_of((2 * core + k) * total, total), rows)]
            for k in range(2)
        ],
        0,
    )
    block = dot(turned, both_ref[:rows, y * 256 : (y + 1) * 256])
    for pair in range(2):
        part = block[:, pair * 128 : (pair + 1) * 128]
        swapped = pltpu.roll(part, 64, 1)
        for z in range(8):
            upper = slice(z * 32, z * 32 + 16)
            lower = slice(z * 32 + 16, z * 32 + 32)
            even = jnp.where(left, part[upper], swapped[lower])
            odd = jnp.where(left, swapped[upper], part[lower])
            for x, tile in ((2 * pair, even), (2 * pair + 1, odd)):
                tiles_ref[x, y % 2, z % 2, y // 2, z // 2] = tile.astype(BF16)


def keep_kernel(length_ref, both_ref, tiles_ref):
    live, _, _ = slot_order(length_ref, length_ref.shape[0])

    def work(rows):
        for y in range(8):
            half_tiles(lax.axis_index("core"), y, both_ref, tiles_ref, rows)

    @pl.when(live <= LIGHT)
    def _():
        work(LIGHT * 64)

    @pl.when(live > LIGHT)
    def _():
        work(both_ref.shape[0] - 128)


def history_kernel(
    length_ref,
    hist_hbm,
    cot_hbm,
    win_hbm,
    both_hbm,
    after_ref,
    out_ref,
    hist_ref,
    cot_ref,
    win_ref,
    dpre_ref,
    grad_ref,
    arrived,
):
    slots, positions, features = hist_ref.shape
    copies = []

    def fetch(source, target):
        copies.append(pltpu.make_async_copy(source, target, arrived.at[len(copies)]))
        copies[-1].start()

    parts = [slice(j * features, (j + 1) * features) for j in range(4)]
    for part in parts:
        fetch(both_hbm.at[: slots * positions, part], dpre_ref.at[:, part])
        fetch(win_hbm.at[:, part], win_ref.at[:, part])
    fetch(hist_hbm, hist_ref)
    fetch(cot_hbm, cot_ref)
    for j, part in enumerate(parts):
        copies[2 * j].wait()
        copies[2 * j + 1].wait()
        share = dot(dpre_ref[:, part], win_ref[:, part], ((1,), (1,)))
        grad_ref[...] = share if j == 0 else grad_ref[...] + share
    copies[-2].wait()
    copies[-1].wait()

    live, places, _ = slot_order(length_ref, slots)
    for i in range(slots):
        place = jnp.where(live <= LIGHT, jnp.minimum(places[i], LIGHT - 1), i)
        at = pl.ds(pl.multiple_of(place * positions, positions), positions)
        normed, scale = normalised(hist_ref[i].astype(F32))
        row = lax.broadcasted_iota(jnp.int32, (positions, features), 0)
        seed = jnp.where(row < length_ref[i], cot_ref[i].astype(F32), 0.0)
        total = seed + norm_backward(grad_ref[at, :], normed, scale)
        out_ref[i] = jnp.where(length_ref[i] > 0, total, 0.0).astype(BF16)


def pair_kernel(one_ref, other_ref, out_ref):
    step = 16

    def add(i, carry):
        at = pl.ds(i * step, step)
        out_ref[at] = (one_ref[at].astype(F32) + other_ref[at].astype(F32)).astype(BF16)
        return carry

    lax.fori_loop(0, out_ref.shape[0] // step, add, 0)


def sum_kernel(parts_ref, out_ref):
    parts, count = parts_ref.shape[:2]
    for i in range(count):
        total = parts_ref[0, i].astype(F32)
        for p in range(1, parts):
            total += parts_ref[p, i].astype(F32)
        out_ref[i] = total.astype(BF16)


def last_kernel(parts_ref, out_ref):
    total = parts_ref[0, 0].astype(F32)
    for p in range(1, parts_ref.shape[0]):
        total += parts_ref[p, 0].astype(F32)
    out_ref[:16, :] = total[:, :64]
    out_ref[16:, :] = total[:, 64:]


VMEM = pl.BlockSpec(memory_space=pltpu.VMEM)
SMEM = pl.BlockSpec(memory_space=pltpu.SMEM)
HBM = pl.BlockSpec(memory_space=pltpu.HBM)
TILES = (4, 2, 2, 4, 4, 16, 128)
ANY = pl.BlockSpec(memory_space=pl.ANY)


def weight_tiles(lengths, hist, cot, w_in, w_out):
    slots, positions, features = hist.shape
    rows = slots * positions
    return pl.pallas_call(
        weight_kernel,
        out_shape=(
            jax.ShapeDtypeStruct(TILES, BF16),
            jax.ShapeDtypeStruct((rows + 128, 4 * features), BF16),
        ),
        in_specs=[SMEM, HBM, HBM, HBM, HBM],
        out_specs=(HBM, HBM),
        scratch_shapes=[
            pltpu.VMEM(TILES, BF16),
            pltpu.VMEM((rows + 128, 4 * features), BF16),
            pltpu.VMEM(hist.shape, BF16),
            pltpu.VMEM(hist.shape, BF16),
            pltpu.VMEM(w_in.shape, BF16),
            pltpu.VMEM(w_out.shape, BF16),
            pltpu.VMEM((rows, features), BF16),
            pltpu.VMEM((rows, features), BF16),
            pltpu.VMEM((rows, 4 * features), BF16),
            pltpu.VMEM((rows, 4 * features), F32),
            pltpu.VMEM((rows, features), F32),
            pltpu.VMEM((rows, features), BF16),
            pltpu.VMEM((rows, features), F32),
            pltpu.VMEM((rows, features), BF16),
            pltpu.VMEM((rows, features), BF16),
            pltpu.VMEM((rows, features), BF16),
            pltpu.SMEM((hist.shape[0],), jnp.int32),
            pltpu.SemaphoreType.DMA((17,)),
            pltpu.SemaphoreType.DMA((36,)),
        ],
        compiler_params=pltpu.CompilerParams(vmem_limit_bytes=56 * 2**20),
        cost_estimate=pl.CostEstimate(
            flops=2 * rows * features * features * 9, bytes_accessed=8 * 2**20, transcendentals=10**6
        ),
    )(lengths, hist, cot, w_in, w_out)


def kept_tiles(lengths, both):
    return pl.pallas_call(
        keep_kernel,
        out_shape=jax.ShapeDtypeStruct(TILES, BF16),
        in_specs=[SMEM, VMEM],
        out_specs=VMEM,
        compiler_params=pltpu.CompilerParams(vmem_limit_bytes=12 * 2**20),
        cost_estimate=pl.CostEstimate(
            flops=both.shape[0] * both.shape[1] * 512,
            bytes_accessed=3 * 2**20,
            transcendentals=0,
        ),
    )(lengths, both)


def history_grads(lengths, hist, cot, w_in, both, after):
    rows = hist.shape[0] * hist.shape[1]
    return pl.pallas_call(
        history_kernel,
        out_shape=jax.ShapeDtypeStruct(hist.shape, BF16),
        in_specs=[SMEM, HBM, HBM, HBM, HBM, ANY],
        out_specs=VMEM,
        scratch_shapes=[
            pltpu.VMEM(hist.shape, BF16),
            pltpu.VMEM(hist.shape, BF16),
            pltpu.VMEM(w_in.shape, BF16),
            pltpu.VMEM((rows, w_in.shape[1]), BF16),
            pltpu.VMEM((rows, hist.shape[-1]), F32),
            pltpu.SemaphoreType.DMA((10,)),
        ],
        compiler_params=pltpu.CompilerParams(vmem_limit_bytes=56 * 2**20),
        cost_estimate=pl.CostEstimate(
            flops=2 * rows * w_in.shape[1] * hist.shape[-1],
            bytes_accessed=6 * 2**20,
            transcendentals=1000,
        ),
    )(lengths, hist, cot, w_in, both, after)


def pair_sum(one, other):
    return pl.pallas_call(
        pair_kernel,
        out_shape=jax.ShapeDtypeStruct(one.shape, BF16),
        in_specs=[VMEM, VMEM],
        out_specs=VMEM,
        compiler_params=pltpu.CompilerParams(vmem_limit_bytes=8 * 2**20),
    )(one, other)


def summed(parts):
    return pl.pallas_call(
        sum_kernel,
        out_shape=jax.ShapeDtypeStruct(parts.shape[1:], BF16),
        in_specs=[VMEM],
        out_specs=VMEM,
        compiler_params=pltpu.CompilerParams(vmem_limit_bytes=8 * 2**20),
    )(parts)


def last_sum(parts):
    return pl.pallas_call(
        last_kernel,
        out_shape=jax.ShapeDtypeStruct((32, 64), F32),
        in_specs=[VMEM],
        out_specs=VMEM,
        compiler_params=pltpu.CompilerParams(vmem_limit_bytes=2 * 2**20),
    )(parts)


def exchanged(tiles, axes):
    return lax.all_to_all(tiles, axes, 0, 0, tiled=True)


def shards(histories, cotangents, lengths, w_in, w_out):
    hist, cot, slot_lengths = histories[0, 0], cotangents[0, 0], lengths[0, 0]
    send, both = weight_tiles(slot_lengths, hist, cot, w_in, w_out)
    other = lax.ppermute(send.reshape(256, 16, 128), "core", [(0, 1), (1, 0)])
    keep = kept_tiles(slot_lengths, both)
    tiles = pair_sum(keep.reshape(256, 16, 128), other)
    tiles = summed(exchanged(tiles.reshape(16, 16, 16, 128), ("x", "yl", "zl")))
    grads = history_grads(slot_lengths, hist, cot, w_in, both, tiles)
    block = last_sum(exchanged(tiles.reshape(16, 1, 16, 128), ("yh", "zh")))
    return (grads[None, None], block)


def solution(mesh):
    torus = Mesh(mesh.devices.reshape(4, 2, 4, 4, 2, 2), AXES)
    seq, rep = ("yh", "yl", "x"), ("zh", "zl", "core")
    placed = (
        P(rep, seq, None, None, None),
        P(rep, seq, None, None, None),
        P(rep, seq, None),
        P(),
        P(),
    )
    return jax.shard_map(
        shards,
        mesh=torus,
        in_specs=placed,
        out_specs=(P(rep, seq, None, None, None), P(rep, seq)),
        check_vma=False,
    )
```
